256 devices in a mesh: row: 8 (over y, core), goal: 32 (over x, z).
Axes of the slice: x: 4, y: 4, z: 8, core: 2. Of those that a mesh axis runs over, the one named last changes fastest.
Arguments:
- phi: bfloat16 [16384, 512], P(('row', 'goal')), may hold values from -100 to 100
- psi: bfloat16 [32768, 512], P(('row', 'goal')), may hold values from -10 to 10
- positives: int32 [16384], P(('row', 'goal')), may hold values from 0 to 32767, as said below
Outputs:
- grad_phi: float32 [16384, 512], P(('row', 'goal'))
- grad_psi: float32 [32768, 512], P(('row', 'goal'))
- loss: float32 [], replicated
The draws below stay inside these ranges and needn't reach their ends.
Inputs may be any that keep to these rules, and one draw needn't show every extreme that they name: `positives`: goal index of each state-action row's positive pair.
All inputs are finite; a program needn't handle non-finite values.
Results may differ from the reference program's by a relative error of at most 0.0055.
Values may be sent and summed in bfloat16 or wider, within the bound.
No kernel may reach another device: no remote copies, remote signals or barrier semaphores. Data moves between devices by JAX's collectives and lax.ppermute only.
A program may use at most 64 MiB of HBM per device.

```python
import math
import jax
import jax.numpy as jnp
from jax import lax

EMBED = 512
ROWS = 16384
GOALS = 32768


def pair_goals(key):
    keyed = jax.random.fold_in(key, 5)
    picks = jax.random.randint(keyed, (ROWS,), 0, GOALS, dtype=jnp.int32)
    return picks.at[0].set(0).at[ROWS - 1].set(GOALS - 1)


def shared_pairs(key):
    picks = pair_goals(key)
    keys = jax.random.split(jax.random.fold_in(key, 11), 8)
    npairs = 16
    goal_step = GOALS // (2 * npairs)
    row_step = ROWS // (2 * npairs)
    goal_pick = jnp.arange(npairs, dtype=jnp.int32) * 2 * goal_step
    row_pick = jnp.arange(npairs, dtype=jnp.int32) * 2 * row_step
    col_scale = jnp.exp(jax.random.uniform(keys[0], (GOALS, 1), jnp.float32, math.log(0.6), math.log(1.6)))
    goal_base = jax.random.normal(keys[1], (GOALS, EMBED), jnp.float32)
    psi = col_scale * goal_base
    psi = psi.at[goal_pick].set(psi[goal_pick])
    psi = psi.at[goal_pick + 1].set(psi[goal_pick + 1])
    row_scale = jnp.exp(jax.random.uniform(keys[6], (ROWS, 1), jnp.float32, math.log(0.3), math.log(3.0)))
    phi = row_scale * jax.random.normal(keys[7], (ROWS, EMBED), jnp.float32) + 0.2 * psi[picks]
    phi = phi.at[row_pick].set(phi[row_pick])
    phi = phi.at[row_pick + 1].set(phi[row_pick + 1])
    return (phi, psi)


def draw_phi(key, part):
    values = shared_pairs(key)[0]
    return jnp.clip(values, -100.0, 100.0).astype(jnp.bfloat16)


def draw_psi(key, part):
    values = shared_pairs(key)[1]
    return jnp.clip(values, -10.0, 10.0).astype(jnp.bfloat16)


def draw_positives(key, part):
    return pair_goals(key)


def setup_inputs(seed: int = 0) -> dict:
    key_of = jax.random.split(jax.random.key(seed), 4)
    return {
        "phi": draw_phi(jax.random.fold_in(key_of[3], 71), 0),
        "psi": draw_psi(jax.random.fold_in(key_of[3], 71), 0),
        "positives": draw_positives(jax.random.fold_in(key_of[3], 71), 0),
    }


def reference(phi, psi, positives):
    scale = 1.0 / math.sqrt(EMBED)
    block = min(512, ROWS)
    count_blocks = ROWS // block
    phi_blocks = phi.reshape(count_blocks, block, EMBED)
    pos_blocks = positives.reshape(count_blocks, block)
    columns = jnp.arange(GOALS, dtype=jnp.int32)

    def forward_step(carry, rows):
        col_max, col_sum = carry
        logits = jnp.dot(rows, psi.T, preferred_element_type=jnp.float32) * scale
        row_max = lax.optimization_barrier(jnp.max(logits, axis=1))
        row_lse = row_max + jnp.log(lax.optimization_barrier(jnp.sum(jnp.exp(logits - row_max[:, None]), axis=1)))
        new_max = jnp.maximum(col_max, lax.optimization_barrier(jnp.max(logits, axis=0)))
        col_sum = col_sum * jnp.exp(col_max - new_max) + lax.optimization_barrier(jnp.sum(jnp.exp(logits - new_max[None, :]), axis=0))
        return ((new_max, col_sum), row_lse)
    start = (jnp.full((GOALS,), -1e+30, jnp.float32), jnp.zeros((GOALS,), jnp.float32))
    (col_max, col_sum), row_lse = lax.scan(forward_step, start, phi_blocks)
    col_lse = col_max + jnp.log(col_sum)
    counts = jnp.zeros((GOALS,), jnp.float32).at[positives].add(1.0)

    def backward_step(carry, item):
        acc, part = carry
        rows, pos, lse = item
        logits = jnp.dot(rows, psi.T, preferred_element_type=jnp.float32) * scale
        hit = pos[:, None] == columns[None, :]
        prob = jnp.exp(logits - lse[:, None]) + counts[None, :] * jnp.exp(logits - col_lse[None, :])
        weights = ((prob - 2.0 * hit.astype(jnp.float32)) * scale).astype(jnp.bfloat16)
        part = part + jnp.sum(jnp.where(hit, col_lse[None, :] - 2.0 * logits, 0.0))
        grad_rows = jnp.dot(weights, psi, preferred_element_type=jnp.float32)
        acc = acc + jnp.dot(weights.T, rows, preferred_element_type=jnp.float32)
        return ((acc, part), grad_rows)
    start = (jnp.zeros((GOALS, EMBED), jnp.float32), jnp.zeros((), jnp.float32))
    (grad_psi, part), grad_rows = lax.scan(backward_step, start, (phi_blocks, pos_blocks, row_lse))
    grad_phi = grad_rows.reshape(ROWS, EMBED)
    loss = (jnp.sum(row_lse) + part) / ROWS
    return (grad_phi, grad_psi, loss)
```

```python
import functools
import math

import jax
import jax.numpy as jnp
from jax import lax
from jax.experimental import pallas as pl
from jax.experimental.pallas import tpu as pltpu
from jax.sharding import Mesh, PartitionSpec as P

ALL = ("y", "core", "x", "z")
PEERS = ("y", "core", "x")
EXTRA = 8
CHUNK = 256
LANES = 128
LOG2E = math.log2(math.e)
SHIFTS = (4, 3, 5, 2, 6, 1, 7)
VMEM_LIMIT = 32 * 1024 * 1024


def nt(left, right):
    return lax.dot_general(
        left, right, (((1,), (1,)), ((), ())), preferred_element_type=jnp.float32
    )


def tn(left, right):
    return lax.dot_general(
        left, right, (((0,), (0,)), ((), ())), preferred_element_type=jnp.float32
    )


def nn(left, right):
    return lax.dot_general(
        left, right, (((1,), (0,)), ((), ())), preferred_element_type=jnp.float32
    )


def to_rows(lanes):
    return jnp.transpose(jnp.broadcast_to(lanes, (LANES, LANES)))


def to_lanes(column):
    return jnp.transpose(jnp.broadcast_to(column, (LANES, LANES)))[0:1]


def place_shards(place_ref, pieces, psi_ref):
    own = place_ref[0]
    shard = pieces[0].shape[0]
    nz = len(pieces)
    for piece, shift in zip(pieces, (0,) + SHIFTS):
        slot = lax.rem(own + nz - shift, nz)
        psi_ref[pl.ds(pl.multiple_of(slot * shard, shard), shard), :] = piece[...]


def row_places(phi_ref, first, shards, shard):
    out = []
    for k in range(shards):
        block = phi_ref[first + k]
        code = to_rows(block[shard : shard + 1, :LANES].astype(jnp.float32))
        out.append(code[:shard] * 256.0 + code[shard : 2 * shard])
    return jnp.concatenate(out, axis=0)


def hit_mask(places, base, ncol):
    rel = places - base
    lane = lax.broadcasted_iota(jnp.int32, rel.shape, 1).astype(jnp.float32)
    off = rel - lane
    return jnp.concatenate(
        [off == float(t * LANES) for t in range(ncol // LANES)], axis=1
    )


def stats_kernel(scale2, shard, place_ref, phi_ref, *refs):
    nz = 1 + len(SHIFTS)
    pieces = refs[:nz]
    row_ref, col_ref, psi_ref = refs[nz:]
    place_shards(place_ref, pieces, psi_ref)
    ncol = psi_ref.shape[0]
    npeer = phi_ref.shape[0]
    per = CHUNK // shard
    base = place_ref[1].astype(jnp.float32)
    psi = psi_ref[...]
    col_max = jnp.full((1, ncol), -1e30, jnp.float32)
    col_sum = jnp.zeros((1, ncol), jnp.float32)
    count = jnp.zeros((1, ncol), jnp.float32)
    hit_sum = jnp.zeros((1, ncol), jnp.float32)
    for c in range(npeer // per):
        rows = phi_ref[c * per : (c + 1) * per, :shard, :].reshape(CHUNK, -1)
        logits = nt(rows, psi) * scale2
        peak = jnp.max(logits, axis=1, keepdims=True)
        total = jnp.sum(jnp.exp2(logits - peak), axis=1, keepdims=True)
        lse = peak + jnp.log2(total)
        for t in range(CHUNK // LANES):
            line = to_lanes(lse[t * LANES : (t + 1) * LANES])
            at = c * (CHUNK // LANES) + t
            row_ref[:, at : at + 1, :] = jnp.broadcast_to(line[None], (npeer, 1, LANES))
        new_max = jnp.maximum(col_max, jnp.max(logits, axis=0, keepdims=True))
        part = jnp.sum(jnp.exp2(logits - new_max), axis=0, keepdims=True)
        col_sum = col_sum * jnp.exp2(col_max - new_max) + part
        col_max = new_max
        hit = hit_mask(row_places(phi_ref, c * per, per, shard), base, ncol)
        count = count + jnp.sum(jnp.where(hit, 1.0, 0.0), axis=0, keepdims=True)
        hit_sum = hit_sum + jnp.sum(jnp.where(hit, logits, 0.0), axis=0, keepdims=True)
    col_lse = col_max + jnp.log2(col_sum)
    nline = ncol // LANES
    hits = jnp.zeros((1, LANES), jnp.float32)
    for t in range(nline):
        cut = slice(t * LANES, (t + 1) * LANES)
        col_ref[t : t + 1, :] = col_lse[:, cut]
        col_ref[nline + t : nline + t + 1, :] = count[:, cut]
        hits = hits + hit_sum[:, cut]
    lines = npeer * shard // LANES
    row_ref[:, lines : lines + 1, :] = jnp.broadcast_to(hits[None], (npeer, 1, LANES))
    row_ref[:, lines + 1 :, :] = jnp.zeros(
        (npeer, row_ref.shape[1] - lines - 1, LANES), jnp.float32
    )


def split3(value):
    first = value.astype(jnp.bfloat16)
    rest = value - first.astype(jnp.float32)
    second = rest.astype(jnp.bfloat16)
    third = (rest - second.astype(jnp.float32)).astype(jnp.bfloat16)
    return jnp.concatenate([first, second, third], axis=0)


def tail_rows(value, width):
    terms = jnp.broadcast_to(value, (1, width))
    first = terms.astype(jnp.bfloat16).astype(jnp.float32)
    second = (terms - first).astype(jnp.bfloat16).astype(jnp.float32)
    third = terms - first - second
    row = lax.broadcasted_iota(jnp.int32, (EXTRA, width), 0)
    full = jnp.where(
        row == 0, first, jnp.where(row == 1, second, jnp.where(row == 2, third, 0.0))
    )
    return full.astype(jnp.bfloat16)


def grads_kernel(scale, scale2, shard, place_ref, phi_ref, rows_ref, *refs):
    nz = 1 + len(SHIFTS)
    pieces = refs[:nz]
    col_parts = refs[nz : 2 * nz]
    gphi_ref = refs[2 * nz]
    gpsi_refs = refs[2 * nz + 1 : 3 * nz + 1]
    psi_ref, acc_ref = refs[3 * nz + 1 :]
    place_shards(place_ref, pieces, psi_ref)
    ncol, width = psi_ref.shape
    npeer = phi_ref.shape[0]
    per = CHUNK // shard
    nline = ncol // LANES
    lines = npeer * shard // LANES
    base = place_ref[1].astype(jnp.float32)
    shift2 = math.log2(scale)

    row_parts = rows_ref[:, :lines, :]
    row_peak = jnp.max(row_parts, axis=0)
    row_lse = row_peak + jnp.log2(jnp.sum(jnp.exp2(row_parts - row_peak[None]), axis=0))
    hits = jnp.sum(rows_ref[:, lines : lines + 1, :], axis=0)
    row_total = jnp.sum(row_lse, keepdims=True) - 2.0 * jnp.sum(hits, keepdims=True)

    cols = [part[...] for part in col_parts]
    col_peak = functools.reduce(jnp.maximum, [part[:nline] for part in cols])
    col_sum = functools.reduce(
        jnp.add, [jnp.exp2(part[:nline] - col_peak) for part in cols]
    )
    counts = functools.reduce(jnp.add, [part[nline:] for part in cols])
    col_lse = col_peak + jnp.log2(col_sum)
    col_total = jnp.sum(counts * col_lse, keepdims=True)
    col_shift = col_lse - jnp.log2(counts) - shift2
    col_line = jnp.concatenate([col_shift[t : t + 1] for t in range(nline)], axis=1)
    row_shift = row_lse - shift2

    psi = psi_ref[...]
    for c in range(npeer // per):
        rows = phi_ref[c * per : (c + 1) * per, :shard, :].reshape(CHUNK, width)
        logits = nt(rows, psi) * scale2
        first = c * (CHUNK // LANES)
        lse = jnp.concatenate(
            [to_rows(row_shift[first + t : first + t + 1]) for t in range(CHUNK // LANES)],
            axis=0,
        )
        lse = jnp.concatenate([lse] * nline, axis=1)
        hit = hit_mask(row_places(phi_ref, c * per, per, shard), base, ncol)
        weights = jnp.exp2(logits - lse) + jnp.exp2(logits - col_line)
        weights = (weights - jnp.where(hit, 2.0 * scale, 0.0)).astype(jnp.bfloat16)
        part = nn(weights, psi).astype(jnp.bfloat16)
        gphi_ref[c * per : (c + 1) * per, :shard, :] = part.reshape(per, shard, width)
        back = tn(weights, rows)
        if c == 0:
            acc_ref[...] = back
        else:
            acc_ref[...] += back
    tail = tail_rows(col_total, width)
    gphi_ref[:, shard:, :] = jnp.broadcast_to(tail[None], (npeer, EXTRA, width))
    tail = tail_rows(row_total, width)
    own = place_ref[0]
    piece = pieces[0].shape[0]
    for out, shift in zip(gpsi_refs, (0,) + SHIFTS):
        slot = lax.rem(own + shift, nz)
        part = acc_ref[pl.ds(pl.multiple_of(slot * piece, piece), piece), :]
        out[:piece, :] = part.astype(jnp.bfloat16)
        out[piece:, :] = tail


def total_kernel(nrow, phi_parts_ref, *refs):
    nz = 1 + len(SHIFTS)
    parts = refs[:nz]
    gphi_ref, gpsi_ref, loss_ref = refs[nz:]
    shard = gphi_ref.shape[0]
    piece = gpsi_ref.shape[0]
    total = phi_parts_ref[0].astype(jnp.float32)
    for k in range(1, phi_parts_ref.shape[0]):
        total = total + phi_parts_ref[k].astype(jnp.float32)
    gphi_ref[...] = total[:shard]
    loss = total[shard : shard + 1, :LANES]
    for r in range(1, 3):
        loss = loss + total[shard + r : shard + r + 1, :LANES]
    total = parts[0][...].astype(jnp.float32)
    for part in parts[1:]:
        total = total + part[...].astype(jnp.float32)
    gpsi_ref[...] = total[:piece]
    for r in range(3):
        loss = loss + total[piece + r : piece + r + 1, :LANES]
    loss_ref[...] = jnp.broadcast_to(loss * (math.log(2.0) / nrow), loss_ref.shape)


def shards(phi, psi, positives):
    shard, width = phi.shape
    piece = psi.shape[0]
    npeer = lax.axis_size(PEERS)
    nz = lax.axis_size("z")
    nrow = npeer * shard
    ncol = nz * piece
    scale = 1.0 / math.sqrt(width)
    scale2 = scale * LOG2E
    peer = lax.axis_index(PEERS)
    place = jnp.stack([lax.axis_index("z"), peer * ncol]).astype(jnp.int32)

    def spread(array):
        return lax.all_to_all(array, PEERS, 0, 0, tiled=True)

    def move(array, shift):
        return lax.ppermute(array, "z", [(i, (i + shift) % nz) for i in range(nz)])

    smem = pl.BlockSpec(memory_space=pltpu.SMEM)
    vmem = pl.BlockSpec(memory_space=pltpu.VMEM)
    params = pltpu.CompilerParams(vmem_limit_bytes=VMEM_LIMIT)

    code = jnp.concatenate([positives // 256, positives % 256]).astype(jnp.bfloat16)
    code = jnp.pad(code[None, :], ((0, EXTRA - 1), (0, width - 2 * shard)))
    block = jnp.concatenate([phi, code], axis=0)
    rows = spread(jnp.broadcast_to(block[None], (npeer,) + block.shape))
    goals = [psi] + [move(psi, s) for s in SHIFTS]

    lines = nrow // LANES + 8
    row_stats, col_stats = pl.pallas_call(
        functools.partial(stats_kernel, scale2, shard),
        out_shape=(
            jax.ShapeDtypeStruct((npeer, lines, LANES), jnp.float32),
            jax.ShapeDtypeStruct((2 * ncol // LANES, LANES), jnp.float32),
        ),
        in_specs=[smem] + [vmem] * (1 + nz),
        out_specs=(vmem, vmem),
        scratch_shapes=[pltpu.VMEM((ncol, width), jnp.bfloat16)],
        compiler_params=params,
        name="stats",
    )(place, rows, *goals)

    row_parts = spread(row_stats)
    col_parts = [col_stats] + [move(col_stats, s) for s in SHIFTS]

    outs = pl.pallas_call(
        functools.partial(grads_kernel, scale, scale2, shard),
        out_shape=(jax.ShapeDtypeStruct((npeer, shard + EXTRA, width), jnp.bfloat16),)
        + (jax.ShapeDtypeStruct((piece + EXTRA, width), jnp.bfloat16),) * nz,
        in_specs=[smem] + [vmem] * (2 + 2 * nz),
        out_specs=(vmem,) * (1 + nz),
        scratch_shapes=[
            pltpu.VMEM((ncol, width), jnp.bfloat16),
            pltpu.VMEM((ncol, width), jnp.float32),
        ],
        compiler_params=params,
        name="grads",
    )(place, rows, row_parts, *goals, *col_parts)

    phi_parts = spread(outs[0])
    psi_parts = [outs[1]] + [move(part, s) for part, s in zip(outs[2:], SHIFTS)]

    grad_phi, grad_psi, loss = pl.pallas_call(
        functools.partial(total_kernel, nrow * nz),
        out_shape=(
            jax.ShapeDtypeStruct((shard, width), jnp.float32),
            jax.ShapeDtypeStruct((piece, width), jnp.float32),
            jax.ShapeDtypeStruct((8, LANES), jnp.float32),
        ),
        in_specs=[vmem] * (1 + nz),
        out_specs=(vmem,) * 3,
        compiler_params=params,
        name="totals",
    )(phi_parts, *psi_parts)
    return (grad_phi, grad_psi, loss[0, 0])


def solution(mesh):
    nrow, ngoal = mesh.shape["row"], mesh.shape["goal"]
    fine = Mesh(mesh.devices.reshape(nrow // 2, 2, ngoal // 8, 8), ALL)
    return jax.shard_map(
        shards,
        mesh=fine,
        in_specs=(P(ALL, None), P(ALL, None), P(ALL)),
        out_specs=(P(ALL, None), P(ALL, None), P()),
        check_vma=False,
    )
```

```python
import functools
import math

import jax
import jax.numpy as jnp
from jax import lax
from jax.experimental import pallas as pl
from jax.experimental.pallas import tpu as pltpu
from jax.sharding import Mesh, PartitionSpec as P

ALL = ("y", "core", "x", "z")
PEERS = ("y", "core", "x")
PLANE = ("y", "x")
EXTRA = 8
CHUNK = 256
LANES = 128
LOG2E = math.log2(math.e)
SHIFTS = (1, 2, 3, 4, 5, 6, 7)
VMEM_LIMIT = 24 * 1024 * 1024


def nt(left, right):
    return lax.dot_general(
        left, right, (((1,), (1,)), ((), ())), preferred_element_type=jnp.float32
    )


def tn(left, right):
    return lax.dot_general(
        left, right, (((0,), (0,)), ((), ())), preferred_element_type=jnp.float32
    )


def nn(left, right):
    return lax.dot_general(
        left, right, (((1,), (0,)), ((), ())), preferred_element_type=jnp.float32
    )


def to_rows(lanes):
    return jnp.transpose(jnp.broadcast_to(lanes, (LANES, LANES)))


def to_lanes(column):
    return jnp.transpose(jnp.broadcast_to(column, (LANES, LANES)))[0:1]


def place_shards(place_ref, pieces, psi_ref):
    own = place_ref[0]
    shard = pieces[0].shape[0]
    nz = len(pieces)
    for piece, shift in zip(pieces, (0,) + SHIFTS):
        slot = lax.rem(own + nz - shift, nz)
        psi_ref[pl.ds(pl.multiple_of(slot * shard, shard), shard), :] = piece[...]


def row_places(phi_ref, first, shards, shard):
    out = []
    for k in range(shards):
        block = phi_ref[first + k]
        code = to_rows(block[shard : shard + 1, :LANES].astype(jnp.float32))
        out.append(code[:shard] * 256.0 + code[shard : 2 * shard])
    return jnp.concatenate(out, axis=0)


def hit_mask(places, base, ncol):
    rel = places - base
    lane = lax.broadcasted_iota(jnp.int32, rel.shape, 1).astype(jnp.float32)
    off = rel - lane
    return jnp.concatenate(
        [off == float(t * LANES) for t in range(ncol // LANES)], axis=1
    )


def pack_kernel(phi_ref, pos_ref, out_ref, block_ref, sem):
    shard, width = phi_ref.shape
    block_ref[:shard, :] = phi_ref[...]
    places = pos_ref[...]
    high = lax.shift_right_logical(places, 8)
    code = jnp.concatenate([high, places - high * 256], axis=1).astype(jnp.float32)
    code = jnp.concatenate([code, jnp.zeros((1, width - 2 * shard), jnp.float32)], axis=1)
    block_ref[shard:, :] = jnp.broadcast_to(code, (EXTRA, width)).astype(jnp.bfloat16)
    copies = [
        pltpu.make_async_copy(block_ref, out_ref.at[k], sem.at[k])
        for k in range(out_ref.shape[0])
    ]
    for copy in copies:
        copy.start()
    for copy in copies:
        copy.wait()


def chunks_of(refs, shard):
    per = CHUNK // shard
    out = []
    for half, ref in enumerate(refs):
        for first in range(0, ref.shape[0], per):
            out.append((len(out), half, first, ref))
    return out


def line_of(place_ref, number, half, count):
    lines = CHUNK // LANES
    core = place_ref[2]
    whose = core if half == 0 else 1 - core
    return whose * (count // 2 * lines) + (number % (count // 2)) * lines


def row_lines(scale2, shard, phi_ref, psi):
    per = CHUNK // shard
    out = []
    for _, _, first, ref in chunks_of((phi_ref,), shard):
        rows = ref[first : first + per, :shard, :].reshape(CHUNK, -1)
        logits = nt(rows, psi) * scale2
        peak = jnp.max(logits, axis=1, keepdims=True)
        total = jnp.sum(jnp.exp2(logits - peak), axis=1, keepdims=True)
        lse = peak + jnp.log2(total)
        for t in range(CHUNK // LANES):
            out.append(to_lanes(lse[t * LANES : (t + 1) * LANES]))
    return jnp.concatenate(out, axis=0)


def own_rows_kernel(scale2, shard, place_ref, phi_ref, *refs):
    pieces = refs[:-4]
    line_ref, psi_out, psi_ref, sem = refs[-4:]
    place_shards(place_ref, pieces, psi_ref)
    copy = pltpu.make_async_copy(psi_ref, psi_out, sem)
    copy.start()
    line_ref[...] = row_lines(scale2, shard, phi_ref, psi_ref[...])
    copy.wait()


def all_rows_kernel(
    scale2, shard, place_ref, phi_ref, line_ref, psi_in, row_ref, psi_ref, sem
):
    copy = pltpu.make_async_copy(psi_in, psi_ref, sem)
    copy.start()
    count = line_ref.shape[0]
    npeer = row_ref.shape[0]
    core = place_ref[2]
    copy.wait()
    lines = row_lines(scale2, shard, phi_ref, psi_ref[...])
    for whose, part in ((core, line_ref[...]), (1 - core, lines)):
        at = pl.multiple_of(whose * count, count)
        row_ref[:, pl.ds(at, count), :] = jnp.broadcast_to(part[None], (npeer, count, LANES))


def block_copies(pairs, sems):
    out = []
    for k, (src, dst) in enumerate(pairs):
        cuts = [pl.ds(r, CHUNK) for r in range(0, src.shape[0], CHUNK)]
        out.append(
            [
                pltpu.make_async_copy(src.at[cut], dst.at[cut], sems.at[k, i])
                for i, cut in enumerate(cuts)
            ]
        )
    return out


def cols_kernel(
    scale2, shard, place_ref, own_ref, other_ref, psi_in, col_ref, peak_ref, exp_out, *refs
):
    psi_ref, exp_ref, sem, sems = refs
    copy = pltpu.make_async_copy(psi_in, psi_ref, sem)
    copy.start()
    nz = col_ref.shape[0]
    ncol = psi_ref.shape[0]
    nline = ncol // LANES
    per = CHUNK // shard
    base = place_ref[1].astype(jnp.float32)
    copy.wait()
    psi = psi_ref[...]
    (stores,) = block_copies([(exp_ref, exp_out)], sems)
    col_max = jnp.full((1, ncol), -1e30, jnp.float32)
    col_sum = jnp.zeros((1, ncol), jnp.float32)
    count = jnp.zeros((1, ncol), jnp.float32)
    hit_sum = jnp.zeros((1, ncol), jnp.float32)
    for number, _, first, phi_ref in chunks_of((own_ref, other_ref), shard):
        rows = phi_ref[first : first + per, :shard, :].reshape(CHUNK, -1)
        logits = nt(rows, psi) * scale2
        new_max = jnp.maximum(col_max, jnp.max(logits, axis=0, keepdims=True))
        part = jnp.exp2(logits - new_max)
        exp_ref[number * CHUNK : (number + 1) * CHUNK, :] = part.astype(jnp.bfloat16)
        stores[number].start()
        part = jnp.sum(part, axis=0, keepdims=True)
        col_sum = col_sum * jnp.exp2(col_max - new_max) + part
        col_max = new_max
        for t in range(nline):
            at = number * nline + t
            peak_ref[at : at + 1, :] = new_max[:, t * LANES : (t + 1) * LANES]
        hit = hit_mask(row_places(phi_ref, first, per, shard), base, ncol)
        count = count + jnp.sum(jnp.where(hit, 1.0, 0.0), axis=0, keepdims=True)
        hit_sum = hit_sum + jnp.sum(jnp.where(hit, logits, 0.0), axis=0, keepdims=True)
    col_lse = col_max + jnp.log2(col_sum)
    for k, line in enumerate((col_lse, count, hit_sum)):
        for t in range(nline):
            cut = line[:, t * LANES : (t + 1) * LANES]
            at = k * nline + t
            col_ref[:, at : at + 1, :] = jnp.broadcast_to(cut[None], (nz, 1, LANES))
    for store in stores:
        store.wait()


def tail_rows(value, width):
    terms = jnp.broadcast_to(value, (1, width))
    first = terms.astype(jnp.bfloat16).astype(jnp.float32)
    second = (terms - first).astype(jnp.bfloat16).astype(jnp.float32)
    third = terms - first - second
    row = lax.broadcasted_iota(jnp.int32, (EXTRA, width), 0)
    full = jnp.where(
        row == 0, first, jnp.where(row == 1, second, jnp.where(row == 2, third, 0.0))
    )
    return full.astype(jnp.bfloat16)


def probs_kernel(
    scale, scale2, shard, place_ref, own_ref, other_ref, psi_in, rows_ref, *refs
):
    prob_out, tail_ref, shift_ref, psi_ref, prob_ref, sem, sems = refs
    copy = pltpu.make_async_copy(psi_in, psi_ref, sem)
    copy.start()
    ncol, width = psi_ref.shape
    per = CHUNK // shard
    base = place_ref[1].astype(jnp.float32)
    row_parts = rows_ref[...]
    row_peak = jnp.max(row_parts, axis=0)
    row_lse = row_peak + jnp.log2(jnp.sum(jnp.exp2(row_parts - row_peak[None]), axis=0))
    tail_ref[...] = tail_rows(jnp.sum(row_lse, keepdims=True), width)
    shift_ref[...] = row_lse - math.log2(scale)
    copy.wait()
    psi = psi_ref[...]
    (stores,) = block_copies([(prob_ref, prob_out)], sems)
    chunks = chunks_of((own_ref, other_ref), shard)
    for number, half, first, phi_ref in chunks:
        rows = phi_ref[first : first + per, :shard, :].reshape(CHUNK, width)
        logits = nt(rows, psi) * scale2
        at = line_of(place_ref, number, half, len(chunks))
        lse = jnp.concatenate(
            [to_rows(shift_ref[pl.ds(at + t, 1), :]) for t in range(CHUNK // LANES)],
            axis=0,
        )
        lse = jnp.concatenate([lse] * (ncol // LANES), axis=1)
        hit = hit_mask(row_places(phi_ref, first, per, shard), base, ncol)
        prob = jnp.exp2(logits - lse) - jnp.where(hit, 2.0 * scale, 0.0)
        prob_ref[number * CHUNK : (number + 1) * CHUNK, :] = prob.astype(jnp.bfloat16)
        stores[number].start()
    for store in stores:
        store.wait()


def weights_kernel(scale, shard, cols_ref, peak_ref, psi_in, prob_in, exp_in, *refs):
    gown_ref, gother_ref, w_ref, psi_ref, prob_ref, exp_ref, sem, sems = refs
    copy = pltpu.make_async_copy(psi_in, psi_ref, sem)
    loads = block_copies([(prob_in, prob_ref), (exp_in, exp_ref)], sems)
    loads[0][0].start()
    loads[1][0].start()
    copy.start()
    for pair in zip(loads[0][1:], loads[1][1:]):
        for load in pair:
            load.start()
    ncol, width = psi_ref.shape
    per = CHUNK // shard
    nline = ncol // LANES
    col_parts = cols_ref[:, :nline, :]
    col_peak = jnp.max(col_parts, axis=0)
    col_lse = col_peak + jnp.log2(jnp.sum(jnp.exp2(col_parts - col_peak[None]), axis=0))
    counts = jnp.sum(cols_ref[:, nline : 2 * nline, :], axis=0)
    hits = jnp.sum(cols_ref[:, 2 * nline :, :], axis=0)
    col_total = jnp.sum(counts * col_lse - 2.0 * hits, keepdims=True)
    tail = jnp.broadcast_to(tail_rows(col_total, width)[None], (per, EXTRA, width))
    copy.wait()
    psi = psi_ref[...]
    plane = gown_ref.shape[0]
    for number in range(len(loads[0])):
        cut = slice(number * CHUNK, (number + 1) * CHUNK)
        peak = peak_ref[number * nline : (number + 1) * nline, :]
        factor = counts * scale * jnp.exp2(peak - col_lse)
        factor = jnp.concatenate([factor[t : t + 1] for t in range(nline)], axis=1)
        loads[0][number].wait()
        loads[1][number].wait()
        weights = exp_ref[cut, :].astype(jnp.float32) * factor
        weights = (prob_ref[cut, :].astype(jnp.float32) + weights).astype(jnp.bfloat16)
        w_ref[cut, :] = weights
        part = nn(weights, psi).astype(jnp.bfloat16)
        half, first = divmod(number * per, plane)
        out_ref = gother_ref if half else gown_ref
        out_ref[first : first + per, :shard, :] = part.reshape(per, shard, width)
        out_ref[first : first + per, shard:, :] = tail


def join_kernel(shard, own_ref, other_ref, out_ref):
    npeer, _, width = own_ref.shape
    for k in range(npeer):
        total = own_ref[k].astype(jnp.float32) + other_ref[k].astype(jnp.float32)
        out_ref[k, :shard, :] = total[:shard].astype(jnp.bfloat16)
        if k == 0:
            loss = jnp.zeros((1, LANES), jnp.float32)
            for r in range(3):
                loss = loss + total[shard + r : shard + r + 1, :LANES]
            tail = tail_rows(loss[:, :1], width)
        out_ref[k, shard:, :] = tail


def goals_kernel(shard, place_ref, w_ref, own_ref, other_ref, tail_ref, *refs):
    nz = 1 + len(SHIFTS)
    gpsi_refs = refs[:nz]
    (acc_ref,) = refs[nz:]
    nrow, ncol = w_ref.shape
    own = own_ref[:, :shard, :].reshape(nrow // 2, -1)
    other = other_ref[:, :shard, :].reshape(nrow // 2, -1)
    rows = jnp.concatenate([own, other], axis=0)
    for c in range(ncol // CHUNK):
        cut = slice(c * CHUNK, (c + 1) * CHUNK)
        acc_ref[cut, :] = tn(w_ref[:, cut], rows).astype(jnp.bfloat16)
    own = place_ref[0]
    piece = ncol // nz
    for out, shift in zip(gpsi_refs, (0,) + SHIFTS):
        slot = lax.rem(own + shift, nz)
        out[:piece, :] = acc_ref[pl.ds(pl.multiple_of(slot * piece, piece), piece), :]
        out[piece:, :] = tail_ref[...]


def relay_kernel(*refs):
    out = refs[-1]
    piece = out.shape[0] - EXTRA
    width = out.shape[1]
    total = refs[0][...].astype(jnp.float32)
    for ref in refs[1:-1]:
        total = total + ref[...].astype(jnp.float32)
    out[:piece, :] = total[:piece].astype(jnp.bfloat16)
    loss = jnp.zeros((1, LANES), jnp.float32)
    for r in range(3):
        loss = loss + total[piece + r : piece + r + 1, :LANES]
    out[piece:, :] = tail_rows(loss[:, :1], width)


def total_kernel(nrow, phi_parts_ref, *refs):
    parts = refs[:-3]
    gphi_ref, gpsi_ref, loss_ref = refs[-3:]
    shard = gphi_ref.shape[0]
    piece = gpsi_ref.shape[0]
    total = phi_parts_ref[0].astype(jnp.float32)
    for k in range(1, phi_parts_ref.shape[0]):
        total = total + phi_parts_ref[k].astype(jnp.float32)
    gphi_ref[...] = total[:shard]
    loss = total[shard : shard + 1, :LANES]
    for r in range(1, 3):
        loss = loss + total[shard + r : shard + r + 1, :LANES]
    total = parts[0][...].astype(jnp.float32)
    for part in parts[1:]:
        total = total + part[...].astype(jnp.float32)
    gpsi_ref[...] = total[:piece]
    for r in range(3):
        loss = loss + total[piece + r : piece + r + 1, :LANES]
    loss_ref[...] = loss[:, :1] * (math.log(2.0) / nrow)


def shards(phi, psi, positives):
    shard, width = phi.shape
    piece = psi.shape[0]
    npeer = lax.axis_size(PEERS)
    nz = lax.axis_size("z")
    nrow = npeer * shard
    ncol = nz * piece
    scale = 1.0 / math.sqrt(width)
    scale2 = scale * LOG2E
    peer = lax.axis_index(PEERS)
    place = jnp.stack(
        [lax.axis_index("z"), peer * ncol, lax.axis_index("core")]
    ).astype(jnp.int32)

    def spread(array, axes):
        return lax.all_to_all(array, axes, 0, 0, tiled=True)

    def swap(array):
        return lax.ppermute(array, "core", [(0, 1), (1, 0)])

    def move(array, shift):
        return lax.ppermute(array, "z", [(i, (i + shift) % nz) for i in range(nz)])

    smem = pl.BlockSpec(memory_space=pltpu.SMEM)
    vmem = pl.BlockSpec(memory_space=pltpu.VMEM)
    params = pltpu.CompilerParams(vmem_limit_bytes=VMEM_LIMIT)

    nplane = npeer // 2
    packed = pl.pallas_call(
        pack_kernel,
        out_shape=jax.ShapeDtypeStruct((nplane, shard + EXTRA, width), jnp.bfloat16),
        in_specs=[vmem] * 2,
        out_specs=pl.BlockSpec(memory_space=pl.ANY),
        scratch_shapes=[
            pltpu.VMEM((shard + EXTRA, width), jnp.bfloat16),
            pltpu.SemaphoreType.DMA((nplane,)),
        ],
        compiler_params=params,
        name="pack",
    )(phi, positives.reshape(1, shard))
    own = spread(packed, PLANE)
    near = {0: psi, 2: move(psi, 2), 6: move(psi, 6), 1: move(psi, 1), 7: move(psi, 7)}
    near[3] = move(near[2], 1)
    near[5] = move(near[6], 7)
    near[4] = move(near[2], 2)
    tied = lax.optimization_barrier((own, *[near[k] for k in range(nz)]))
    own = tied[0]
    near = dict(enumerate(tied[1:]))
    other = swap(own)
    goals = [near[k] for k in range(nz)]
    flops = 2 * nrow * ncol * width

    def cost(products):
        return pl.CostEstimate(
            flops=int(products * flops), bytes_accessed=4 << 20, transcendentals=int(products * nrow * ncol)
        )

    anywhere = pl.BlockSpec(memory_space=pl.ANY)
    hbm = pl.BlockSpec(memory_space=pltpu.HBM)
    dma = pltpu.SemaphoreType.DMA
    nchunk = nrow // CHUNK
    psi_scratch = pltpu.VMEM((ncol, width), jnp.bfloat16)
    tile = jax.ShapeDtypeStruct((nrow, ncol), jnp.bfloat16)
    tile_hbm = pltpu.HBM((nrow, ncol), jnp.bfloat16)
    tile_scratch = pltpu.VMEM((nrow, ncol), jnp.bfloat16)
    own_lines, psi_all = pl.pallas_call(
        functools.partial(own_rows_kernel, scale2, shard),
        out_shape=(
            jax.ShapeDtypeStruct((nrow // LANES // 2, LANES), jnp.float32),
            jax.ShapeDtypeStruct((ncol, width), jnp.bfloat16),
        ),
        in_specs=[smem] + [vmem] * (1 + nz),
        out_specs=(vmem, anywhere),
        scratch_shapes=[psi_scratch, dma],
        compiler_params=params,
        cost_estimate=cost(0.5),
        name="own_rows",
    )(place, own, *goals)
    row_stats = pl.pallas_call(
        functools.partial(all_rows_kernel, scale2, shard),
        out_shape=jax.ShapeDtypeStruct((npeer, nrow // LANES, LANES), jnp.float32),
        in_specs=[smem] + [vmem] * 2 + [anywhere],
        out_specs=vmem,
        scratch_shapes=[psi_scratch, dma],
        compiler_params=params,
        cost_estimate=cost(0.5),
        name="all_rows",
    )(place, other, own_lines, psi_all)
    row_parts = spread(row_stats, PEERS)

    col_stats, peaks, exps = pl.pallas_call(
        functools.partial(cols_kernel, scale2, shard),
        out_shape=(
            jax.ShapeDtypeStruct((nz, 3 * ncol // LANES, LANES), jnp.float32),
            jax.ShapeDtypeStruct((nchunk * ncol // LANES, LANES), jnp.float32),
            tile_hbm,
        ),
        in_specs=[smem] + [vmem] * 2 + [anywhere],
        out_specs=(vmem, vmem, hbm),
        scratch_shapes=[psi_scratch, tile_scratch, dma, dma((1, nchunk))],
        compiler_params=params,
        cost_estimate=cost(1),
        name="cols",
    )(place, own, other, psi_all)
    row_parts, col_stats = lax.optimization_barrier((row_parts, col_stats))
    col_parts = spread(col_stats, "z")

    probs, tail = pl.pallas_call(
        functools.partial(probs_kernel, scale, scale2, shard),
        out_shape=(tile_hbm, jax.ShapeDtypeStruct((EXTRA, width), jnp.bfloat16)),
        in_specs=[smem] + [vmem] * 2 + [anywhere, vmem],
        out_specs=(hbm, vmem),
        scratch_shapes=[
            pltpu.VMEM((nrow // LANES, LANES), jnp.float32),
            psi_scratch,
            tile_scratch,
            dma,
            dma((1, nchunk)),
        ],
        compiler_params=params,
        cost_estimate=cost(1),
        name="probs",
    )(place, own, other, psi_all, row_parts)

    half = jax.ShapeDtypeStruct((nplane, shard + EXTRA, width), jnp.bfloat16)
    gown, gother, weights = pl.pallas_call(
        functools.partial(weights_kernel, scale, shard),
        out_shape=(half, half, tile),
        in_specs=[vmem] * 2 + [anywhere, hbm, hbm],
        out_specs=(vmem,) * 3,
        scratch_shapes=[psi_scratch, tile_scratch, tile_scratch, dma, dma((2, nchunk))],
        compiler_params=params,
        cost_estimate=cost(1),
        name="weights",
    )(
        col_parts,
        peaks,
        psi_all,
        pltpu.with_memory_space_constraint(probs, pltpu.HBM),
        pltpu.with_memory_space_constraint(exps, pltpu.HBM),
    )
    part = jax.ShapeDtypeStruct((piece + EXTRA, width), jnp.bfloat16)
    gpsi = pl.pallas_call(
        functools.partial(goals_kernel, shard),
        out_shape=(part,) * nz,
        in_specs=[smem] + [vmem] * 4,
        out_specs=(vmem,) * nz,
        scratch_shapes=[pltpu.VMEM((ncol, width), jnp.bfloat16)],
        compiler_params=params,
        cost_estimate=cost(1),
        name="goals",
    )(place, weights, own, other, tail)

    other_part, *gpsi = lax.optimization_barrier((swap(gother), *gpsi))
    joined = pl.pallas_call(
        functools.partial(join_kernel, shard),
        out_shape=half,
        in_specs=[vmem] * 2,
        out_specs=vmem,
        compiler_params=params,
        name="join",
    )(gown, other_part)
    phi_parts = spread(joined, PLANE)

    def relay(*parts):
        return pl.pallas_call(
            relay_kernel,
            out_shape=part,
            in_specs=[vmem] * len(parts),
            out_specs=vmem,
            compiler_params=params,
            name="relay",
        )(*parts)

    over3, over4, over5 = move(gpsi[3], 1), move(gpsi[4], 2), move(gpsi[5], 7)
    psi_parts = [gpsi[0], move(gpsi[1], 1), move(gpsi[7], 7)]
    psi_parts.append(move(relay(gpsi[2], over3, over4), 2))
    psi_parts.append(move(relay(gpsi[6], over5), 6))

    grad_phi, grad_psi, loss = pl.pallas_call(
        functools.partial(total_kernel, nrow * nz),
        out_shape=(
            jax.ShapeDtypeStruct((shard, width), jnp.float32),
            jax.ShapeDtypeStruct((piece, width), jnp.float32),
            jax.ShapeDtypeStruct((1, 1), jnp.float32),
        ),
        in_specs=[vmem] * (1 + len(psi_parts)),
        out_specs=(vmem,) * 3,
        compiler_params=params,
        name="totals",
    )(phi_parts, *psi_parts)
    return (grad_phi, grad_psi, loss.reshape(()))


def solution(mesh):
    nrow, ngoal = mesh.shape["row"], mesh.shape["goal"]
    fine = Mesh(mesh.devices.reshape(nrow // 2, 2, ngoal // 8, 8), ALL)
    return jax.shard_map(
        shards,
        mesh=fine,
        in_specs=(P(ALL, None), P(ALL, None), P(ALL)),
        out_specs=(P(ALL, None), P(ALL, None), P()),
        check_vma=False,
    )
```

```python
import functools
import math

import jax
import jax.numpy as jnp
from jax import lax
from jax.experimental import pallas as pl
from jax.experimental.pallas import tpu as pltpu
from jax.sharding import Mesh, PartitionSpec as P

ALL = ("y", "core", "x", "z")
PEERS = ("y", "core", "x")
PLANE = ("y", "x")
EXTRA = 8
CHUNK = 256
LANES = 128
LOG2E = math.log2(math.e)
SHIFTS = (1, 2, 3, 4, 5, 6, 7)
VMEM_LIMIT = 24 * 1024 * 1024


def nt(left, right):
    return lax.dot_general(
        left, right, (((1,), (1,)), ((), ())), preferred_element_type=jnp.float32
    )


def tn(left, right):
    return lax.dot_general(
        left, right, (((0,), (0,)), ((), ())), preferred_element_type=jnp.float32
    )


def nn(left, right):
    return lax.dot_general(
        left, right, (((1,), (0,)), ((), ())), preferred_element_type=jnp.float32
    )


def to_rows(lanes):
    return jnp.transpose(jnp.broadcast_to(lanes, (LANES, LANES)))


def to_lanes(column):
    return jnp.transpose(jnp.broadcast_to(column, (LANES, LANES)))[0:1]


def place_shards(place_ref, pieces, psi_ref):
    own = place_ref[0]
    shard = pieces[0].shape[0]
    nz = len(pieces)
    for piece, shift in zip(pieces, (0,) + SHIFTS):
        slot = lax.rem(own + nz - shift, nz)
        psi_ref[pl.ds(pl.multiple_of(slot * shard, shard), shard), :] = piece[...]


def row_places(phi_ref, first, shards, shard):
    out = []
    for k in range(shards):
        block = phi_ref[first + k]
        code = to_rows(block[shard : shard + 1, :LANES].astype(jnp.float32))
        out.append(code[:shard] * 256.0 + code[shard : 2 * shard])
    return jnp.concatenate(out, axis=0)


def hit_mask(places, base, ncol):
    rel = places - base
    lane = lax.broadcasted_iota(jnp.int32, rel.shape, 1).astype(jnp.float32)
    off = rel - lane
    return jnp.concatenate(
        [off == float(t * LANES) for t in range(ncol // LANES)], axis=1
    )


def pack_kernel(phi_in, pos_in, out_ref, block_ref, pos_ref, sems, sem):
    shard, width = phi_in.shape
    loads = [
        pltpu.make_async_copy(pos_in, pos_ref, sems.at[0]),
        pltpu.make_async_copy(phi_in, block_ref.at[:shard], sems.at[1]),
    ]
    for load in loads:
        load.start()
    loads[0].wait()
    places = pos_ref[...]
    high = lax.shift_right_logical(places, 8)
    code = jnp.concatenate([high, places - high * 256], axis=1).astype(jnp.float32)
    code = jnp.concatenate([code, jnp.zeros((1, width - 2 * shard), jnp.float32)], axis=1)
    block_ref[shard:, :] = jnp.broadcast_to(code, (EXTRA, width)).astype(jnp.bfloat16)
    loads[1].wait()
    copies = [
        pltpu.make_async_copy(block_ref, out_ref.at[k], sem.at[k])
        for k in range(out_ref.shape[0])
    ]
    for copy in copies:
        copy.start()
    for copy in copies:
        copy.wait()


def chunks_of(refs, shard):
    per = CHUNK // shard
    out = []
    for half, ref in enumerate(refs):
        for first in range(0, ref.shape[0], per):
            out.append((len(out), half, first, ref))
    return out


def line_of(place_ref, number, half, count):
    lines = CHUNK // LANES
    core = place_ref[2]
    whose = core if half == 0 else 1 - core
    return whose * (count // 2 * lines) + (number % (count // 2)) * lines


def row_lines(scale2, shard, phi_ref, psi):
    per = CHUNK // shard
    out = []
    for _, _, first, ref in chunks_of((phi_ref,), shard):
        rows = ref[first : first + per, :shard, :].reshape(CHUNK, -1)
        logits = nt(rows, psi) * scale2
        peak = jnp.max(logits, axis=1, keepdims=True)
        total = jnp.sum(jnp.exp2(logits - peak), axis=1, keepdims=True)
        lse = peak + jnp.log2(total)
        for t in range(CHUNK // LANES):
            out.append(to_lanes(lse[t * LANES : (t + 1) * LANES]))
    return jnp.concatenate(out, axis=0)


def own_rows_kernel(scale2, shard, place_ref, phi_ref, *refs):
    pieces = refs[:-4]
    line_ref, psi_out, psi_ref, sem = refs[-4:]
    place_shards(place_ref, pieces, psi_ref)
    copy = pltpu.make_async_copy(psi_ref, psi_out, sem)
    copy.start()
    line_ref[...] = row_lines(scale2, shard, phi_ref, psi_ref[...])
    copy.wait()


def all_rows_kernel(
    scale2, shard, place_ref, phi_ref, line_ref, psi_in, row_ref, psi_ref, sem
):
    copy = pltpu.make_async_copy(psi_in, psi_ref, sem)
    copy.start()
    count = line_ref.shape[0]
    npeer = row_ref.shape[0]
    core = place_ref[2]
    copy.wait()
    lines = row_lines(scale2, shard, phi_ref, psi_ref[...])
    for whose, part in ((core, line_ref[...]), (1 - core, lines)):
        at = pl.multiple_of(whose * count, count)
        row_ref[:, pl.ds(at, count), :] = jnp.broadcast_to(part[None], (npeer, count, LANES))


def block_copies(pairs, sems):
    out = []
    for k, (src, dst) in enumerate(pairs):
        cuts = [pl.ds(r, CHUNK) for r in range(0, src.shape[0], CHUNK)]
        out.append(
            [
                pltpu.make_async_copy(src.at[cut], dst.at[cut], sems.at[k, i])
                for i, cut in enumerate(cuts)
            ]
        )
    return out


def cols_kernel(
    scale2, shard, place_ref, own_ref, other_ref, psi_in, col_ref, peak_ref, psi_ref, sem
):
    copy = pltpu.make_async_copy(psi_in, psi_ref, sem)
    copy.start()
    nz = col_ref.shape[0]
    ncol = psi_ref.shape[0]
    nline = ncol // LANES
    per = CHUNK // shard
    base = place_ref[1].astype(jnp.float32)
    lane = lax.broadcasted_iota(jnp.int32, (CHUNK, LANES), 1).astype(jnp.float32)
    copy.wait()
    psi = psi_ref[...]
    col_max = jnp.full((1, ncol), -1e30, jnp.float32)
    col_sum = jnp.zeros((1, ncol), jnp.float32)
    count = jnp.zeros((LANES, LANES), jnp.float32)
    hit_sum = jnp.zeros((1, ncol), jnp.float32)
    for _, _, first, phi_ref in chunks_of((own_ref, other_ref), shard):
        rows = phi_ref[first : first + per, :shard, :].reshape(CHUNK, -1)
        logits = nt(rows, psi) * scale2
        new_max = jnp.maximum(col_max, jnp.max(logits, axis=0, keepdims=True))
        part = jnp.sum(jnp.exp2(logits - new_max), axis=0, keepdims=True)
        col_sum = col_sum * jnp.exp2(col_max - new_max) + part
        col_max = new_max
        places = row_places(phi_ref, first, per, shard)
        hit = hit_mask(places, base, ncol)
        hit_sum = hit_sum + jnp.sum(jnp.where(hit, logits, 0.0), axis=0, keepdims=True)
        high = jnp.floor((places - base) * (1.0 / LANES))
        low = places - base - high * LANES
        high = jnp.where(high == lane, 1.0, 0.0).astype(jnp.bfloat16)
        low = jnp.where(low == lane, 1.0, 0.0).astype(jnp.bfloat16)
        count = count + tn(high, low)
    col_lse = col_max + jnp.log2(col_sum)
    for k, line in enumerate((col_lse, hit_sum)):
        for t in range(nline):
            cut = line[:, t * LANES : (t + 1) * LANES]
            at = 2 * k * nline + t
            col_ref[:, at : at + 1, :] = jnp.broadcast_to(cut[None], (nz, 1, LANES))
    for t in range(nline):
        peak_ref[t : t + 1, :] = col_max[:, t * LANES : (t + 1) * LANES]
    col_ref[:, nline : 2 * nline, :] = jnp.broadcast_to(
        count[None, :nline, :], (nz, nline, LANES)
    )


def tail_rows(value, width):
    terms = jnp.broadcast_to(value, (1, width))
    first = terms.astype(jnp.bfloat16).astype(jnp.float32)
    second = (terms - first).astype(jnp.bfloat16).astype(jnp.float32)
    third = terms - first - second
    row = lax.broadcasted_iota(jnp.int32, (EXTRA, width), 0)
    full = jnp.where(
        row == 0, first, jnp.where(row == 1, second, jnp.where(row == 2, third, 0.0))
    )
    return full.astype(jnp.bfloat16)


def probs_kernel(
    scale, scale2, shard, place_ref, own_ref, other_ref, psi_in, rows_ref, peak_ref, *refs
):
    prob_out, exp_out, tail_ref, shift_ref, psi_ref, prob_ref, exp_ref, sem, sems = refs
    copy = pltpu.make_async_copy(psi_in, psi_ref, sem)
    copy.start()
    ncol, width = psi_ref.shape
    per = CHUNK // shard
    base = place_ref[1].astype(jnp.float32)
    row_parts = rows_ref[...]
    row_peak = jnp.max(row_parts, axis=0)
    row_lse = row_peak + jnp.log2(jnp.sum(jnp.exp2(row_parts - row_peak[None]), axis=0))
    tail_ref[...] = tail_rows(jnp.sum(row_lse, keepdims=True), width)
    shift_ref[...] = row_lse - math.log2(scale)
    copy.wait()
    psi = psi_ref[...]
    prob_stores, exp_stores = block_copies([(prob_ref, prob_out), (exp_ref, exp_out)], sems)
    peak = jnp.concatenate([peak_ref[t : t + 1] for t in range(ncol // LANES)], axis=1)
    chunks = chunks_of((own_ref, other_ref), shard)
    for number, half, first, phi_ref in chunks:
        rows = phi_ref[first : first + per, :shard, :].reshape(CHUNK, width)
        logits = nt(rows, psi) * scale2
        at = line_of(place_ref, number, half, len(chunks))
        lse = jnp.concatenate(
            [to_rows(shift_ref[pl.ds(at + t, 1), :]) for t in range(CHUNK // LANES)],
            axis=0,
        )
        lse = jnp.concatenate([lse] * (ncol // LANES), axis=1)
        hit = hit_mask(row_places(phi_ref, first, per, shard), base, ncol)
        prob = jnp.exp2(logits - lse) - jnp.where(hit, 2.0 * scale, 0.0)
        prob_ref[number * CHUNK : (number + 1) * CHUNK, :] = prob.astype(jnp.bfloat16)
        prob_stores[number].start()
        part = jnp.exp2(logits - peak).astype(jnp.bfloat16)
        exp_ref[number * CHUNK : (number + 1) * CHUNK, :] = part
        exp_stores[number].start()
    for store in prob_stores + exp_stores:
        store.wait()


def weights_kernel(scale, shard, cols_ref, peak_ref, psi_in, prob_in, exp_in, *refs):
    gown_ref, gother_ref, w_ref, psi_ref, prob_ref, exp_ref, sem, sems = refs
    copy = pltpu.make_async_copy(psi_in, psi_ref, sem)
    loads = block_copies([(prob_in, prob_ref), (exp_in, exp_ref)], sems)
    loads[0][0].start()
    loads[1][0].start()
    copy.start()
    for pair in zip(loads[0][1:], loads[1][1:]):
        for load in pair:
            load.start()
    ncol, width = psi_ref.shape
    per = CHUNK // shard
    nline = ncol // LANES
    col_parts = cols_ref[:, :nline, :]
    col_peak = jnp.max(col_parts, axis=0)
    col_lse = col_peak + jnp.log2(jnp.sum(jnp.exp2(col_parts - col_peak[None]), axis=0))
    counts = jnp.sum(cols_ref[:, nline : 2 * nline, :], axis=0)
    hits = jnp.sum(cols_ref[:, 2 * nline :, :], axis=0)
    col_total = jnp.sum(counts * col_lse - 2.0 * hits, keepdims=True)
    tail = jnp.broadcast_to(tail_rows(col_total, width)[None], (per, EXTRA, width))
    factor = counts * scale * jnp.exp2(peak_ref[...] - col_lse)
    factor = jnp.concatenate([factor[t : t + 1] for t in range(nline)], axis=1)
    copy.wait()
    psi = psi_ref[...]
    plane = gown_ref.shape[0]
    for number in range(len(loads[0])):
        cut = slice(number * CHUNK, (number + 1) * CHUNK)
        loads[0][number].wait()
        loads[1][number].wait()
        weights = exp_ref[cut, :].astype(jnp.float32) * factor
        weights = (prob_ref[cut, :].astype(jnp.float32) + weights).astype(jnp.bfloat16)
        w_ref[cut, :] = weights
        part = nn(weights, psi).astype(jnp.bfloat16)
        half, first = divmod(number * per, plane)
        out_ref = gother_ref if half else gown_ref
        out_ref[first : first + per, :shard, :] = part.reshape(per, shard, width)
        out_ref[first : first + per, shard:, :] = tail


def join_kernel(shard, own_ref, other_ref, out_ref):
    npeer, _, width = own_ref.shape
    for k in range(npeer):
        total = own_ref[k].astype(jnp.float32) + other_ref[k].astype(jnp.float32)
        out_ref[k, :shard, :] = total[:shard].astype(jnp.bfloat16)
        if k == 0:
            loss = jnp.zeros((1, LANES), jnp.float32)
            for r in range(3):
                loss = loss + total[shard + r : shard + r + 1, :LANES]
            tail = tail_rows(loss[:, :1], width)
        out_ref[k, shard:, :] = tail


def goals_kernel(shard, place_ref, w_ref, own_ref, other_ref, tail_ref, *refs):
    nz = 1 + len(SHIFTS)
    gpsi_refs = refs[:nz]
    (acc_ref,) = refs[nz:]
    nrow, ncol = w_ref.shape
    own = own_ref[:, :shard, :].reshape(nrow // 2, -1)
    other = other_ref[:, :shard, :].reshape(nrow // 2, -1)
    rows = jnp.concatenate([own, other], axis=0)
    for c in range(ncol // CHUNK):
        cut = slice(c * CHUNK, (c + 1) * CHUNK)
        acc_ref[cut, :] = tn(w_ref[:, cut], rows).astype(jnp.bfloat16)
    own = place_ref[0]
    piece = ncol // nz
    for out, shift in zip(gpsi_refs, (0,) + SHIFTS):
        slot = lax.rem(own + shift, nz)
        out[:piece, :] = acc_ref[pl.ds(pl.multiple_of(slot * piece, piece), piece), :]
        out[piece:, :] = tail_ref[...]


def relay_kernel(parity, place_ref, *refs):
    out = refs[-1]
    piece = out.shape[0] - EXTRA
    width = out.shape[1]
    total = refs[0][...].astype(jnp.float32)
    for ref in refs[1:-2]:
        total = total + ref[...].astype(jnp.float32)
    counts = lax.rem(place_ref[0], 2) == parity
    total = total + jnp.where(counts, refs[-2][...].astype(jnp.float32), 0.0)
    out[:piece, :] = total[:piece].astype(jnp.bfloat16)
    loss = jnp.zeros((1, LANES), jnp.float32)
    for r in range(3):
        loss = loss + total[piece + r : piece + r + 1, :LANES]
    out[piece:, :] = tail_rows(loss[:, :1], width)


def total_kernel(nrow, phi_parts_ref, *refs):
    parts = refs[:-3]
    gphi_ref, gpsi_ref, loss_ref = refs[-3:]
    shard = gphi_ref.shape[0]
    piece = gpsi_ref.shape[0]
    total = phi_parts_ref[0].astype(jnp.float32)
    for k in range(1, phi_parts_ref.shape[0]):
        total = total + phi_parts_ref[k].astype(jnp.float32)
    gphi_ref[...] = total[:shard]
    loss = total[shard : shard + 1, :LANES]
    for r in range(1, 3):
        loss = loss + total[shard + r : shard + r + 1, :LANES]
    total = parts[0][...].astype(jnp.float32)
    for part in parts[1:]:
        total = total + part[...].astype(jnp.float32)
    gpsi_ref[...] = total[:piece]
    for r in range(3):
        loss = loss + total[piece + r : piece + r + 1, :LANES]
    loss_ref[...] = loss[:, :1] * (math.log(2.0) / nrow)


def shards(phi, psi, positives):
    shard, width = phi.shape
    piece = psi.shape[0]
    npeer = lax.axis_size(PEERS)
    nz = lax.axis_size("z")
    nrow = npeer * shard
    ncol = nz * piece
    scale = 1.0 / math.sqrt(width)
    scale2 = scale * LOG2E
    peer = lax.axis_index(PEERS)
    place = jnp.stack(
        [lax.axis_index("z"), peer * ncol, lax.axis_index("core")]
    ).astype(jnp.int32)

    def spread(array, axes):
        return lax.all_to_all(array, axes, 0, 0, tiled=True)

    def swap(array):
        return lax.ppermute(array, "core", [(0, 1), (1, 0)])

    def move(array, shift):
        return lax.ppermute(array, "z", [(i, (i + shift) % nz) for i in range(nz)])

    smem = pl.BlockSpec(memory_space=pltpu.SMEM)
    vmem = pl.BlockSpec(memory_space=pltpu.VMEM)
    hbm = pl.BlockSpec(memory_space=pltpu.HBM)
    params = pltpu.CompilerParams(vmem_limit_bytes=VMEM_LIMIT)

    nplane = npeer // 2
    packed = pl.pallas_call(
        pack_kernel,
        out_shape=pltpu.HBM((nplane, shard + EXTRA, width), jnp.bfloat16),
        in_specs=[hbm] * 2,
        out_specs=hbm,
        scratch_shapes=[
            pltpu.VMEM((shard + EXTRA, width), jnp.bfloat16),
            pltpu.VMEM((1, shard), jnp.int32),
            pltpu.SemaphoreType.DMA((2,)),
            pltpu.SemaphoreType.DMA((nplane,)),
        ],
        compiler_params=params,
        name="pack",
    )(
        pltpu.with_memory_space_constraint(phi, pltpu.HBM),
        pltpu.with_memory_space_constraint(positives.reshape(1, shard), pltpu.HBM),
    )
    own = spread(packed, PLANE)
    near = {0: psi, 2: move(psi, 2), 6: move(psi, 6), 1: move(psi, 1), 7: move(psi, 7)}
    near[3] = move(near[2], 1)
    near[5] = move(near[6], 7)
    even = lax.rem(lax.axis_index("z"), 2) == 0
    across = [(i, (i + (2 if i % 2 == 0 else 6)) % nz) for i in range(nz)]
    near[4] = lax.ppermute(jnp.where(even, near[2], near[6]), "z", across)
    tied = lax.optimization_barrier((own, *[near[k] for k in range(nz)]))
    own = tied[0]
    near = dict(enumerate(tied[1:]))
    other = swap(own)
    goals = [near[k] for k in range(nz)]
    flops = 2 * nrow * ncol * width

    def cost(products):
        return pl.CostEstimate(
            flops=int(products * flops), bytes_accessed=4 << 20, transcendentals=int(products * nrow * ncol)
        )

    anywhere = pl.BlockSpec(memory_space=pl.ANY)
    dma = pltpu.SemaphoreType.DMA
    nchunk = nrow // CHUNK
    psi_scratch = pltpu.VMEM((ncol, width), jnp.bfloat16)
    tile = jax.ShapeDtypeStruct((nrow, ncol), jnp.bfloat16)
    tile_hbm = pltpu.HBM((nrow, ncol), jnp.bfloat16)
    tile_scratch = pltpu.VMEM((nrow, ncol), jnp.bfloat16)
    own_lines, psi_all = pl.pallas_call(
        functools.partial(own_rows_kernel, scale2, shard),
        out_shape=(
            jax.ShapeDtypeStruct((nrow // LANES // 2, LANES), jnp.float32),
            jax.ShapeDtypeStruct((ncol, width), jnp.bfloat16),
        ),
        in_specs=[smem] + [vmem] * (1 + nz),
        out_specs=(vmem, anywhere),
        scratch_shapes=[psi_scratch, dma],
        compiler_params=params,
        cost_estimate=cost(0.5),
        name="own_rows",
    )(place, own, *goals)
    row_stats = pl.pallas_call(
        functools.partial(all_rows_kernel, scale2, shard),
        out_shape=jax.ShapeDtypeStruct((npeer, nrow // LANES, LANES), jnp.float32),
        in_specs=[smem] + [vmem] * 2 + [anywhere],
        out_specs=vmem,
        scratch_shapes=[psi_scratch, dma],
        compiler_params=params,
        cost_estimate=cost(0.5),
        name="all_rows",
    )(place, other, own_lines, psi_all)
    row_parts = spread(row_stats, PEERS)

    col_stats, peaks = pl.pallas_call(
        functools.partial(cols_kernel, scale2, shard),
        out_shape=(
            jax.ShapeDtypeStruct((nz, 3 * ncol // LANES, LANES), jnp.float32),
            jax.ShapeDtypeStruct((ncol // LANES, LANES), jnp.float32),
        ),
        in_specs=[smem] + [vmem] * 2 + [anywhere],
        out_specs=(vmem, vmem),
        scratch_shapes=[psi_scratch, dma],
        compiler_params=params,
        cost_estimate=cost(1),
        name="cols",
    )(place, own, other, psi_all)
    row_parts, col_stats = lax.optimization_barrier((row_parts, col_stats))
    col_parts = spread(col_stats, "z")

    probs, exps, tail = pl.pallas_call(
        functools.partial(probs_kernel, scale, scale2, shard),
        out_shape=(tile_hbm, tile_hbm, jax.ShapeDtypeStruct((EXTRA, width), jnp.bfloat16)),
        in_specs=[smem] + [vmem] * 2 + [anywhere, vmem, vmem],
        out_specs=(hbm, hbm, vmem),
        scratch_shapes=[
            pltpu.VMEM((nrow // LANES, LANES), jnp.float32),
            psi_scratch,
            tile_scratch,
            tile_scratch,
            dma,
            dma((2, nchunk)),
        ],
        compiler_params=params,
        cost_estimate=cost(1),
        name="probs",
    )(place, own, other, psi_all, row_parts, peaks)

    half = jax.ShapeDtypeStruct((nplane, shard + EXTRA, width), jnp.bfloat16)
    gown, gother, weights = pl.pallas_call(
        functools.partial(weights_kernel, scale, shard),
        out_shape=(half, half, tile),
        in_specs=[vmem] * 2 + [anywhere, hbm, hbm],
        out_specs=(vmem,) * 3,
        scratch_shapes=[psi_scratch, tile_scratch, tile_scratch, dma, dma((2, nchunk))],
        compiler_params=params,
        cost_estimate=cost(1),
        name="weights",
    )(
        col_parts,
        peaks,
        psi_all,
        pltpu.with_memory_space_constraint(probs, pltpu.HBM),
        pltpu.with_memory_space_constraint(exps, pltpu.HBM),
    )
    part = jax.ShapeDtypeStruct((piece + EXTRA, width), jnp.bfloat16)
    gpsi = pl.pallas_call(
        functools.partial(goals_kernel, shard),
        out_shape=(part,) * nz,
        in_specs=[smem] + [vmem] * 4,
        out_specs=(vmem,) * nz,
        scratch_shapes=[pltpu.VMEM((ncol, width), jnp.bfloat16)],
        compiler_params=params,
        cost_estimate=cost(1),
        name="goals",
    )(place, weights, own, other, tail)

    other_part, *gpsi = lax.optimization_barrier((swap(gother), *gpsi))
    joined = pl.pallas_call(
        functools.partial(join_kernel, shard),
        out_shape=half,
        in_specs=[vmem] * 2,
        out_specs=vmem,
        compiler_params=params,
        name="join",
    )(gown, other_part)
    phi_parts = spread(joined, PLANE)

    def relay(parity, *parts):
        return pl.pallas_call(
            functools.partial(relay_kernel, parity),
            out_shape=part,
            in_specs=[smem] + [vmem] * len(parts),
            out_specs=vmem,
            compiler_params=params,
            name="relay",
        )(place, *parts)

    over3, over5 = move(gpsi[3], 1), move(gpsi[5], 7)
    over4 = lax.ppermute(gpsi[4], "z", across)
    psi_parts = [gpsi[0], move(gpsi[1], 1), move(gpsi[7], 7)]
    psi_parts.append(move(relay(0, gpsi[2], over3, over4), 2))
    psi_parts.append(move(relay(1, gpsi[6], over5, over4), 6))

    grad_phi, grad_psi, loss = pl.pallas_call(
        functools.partial(total_kernel, nrow * nz),
        out_shape=(
            jax.ShapeDtypeStruct((shard, width), jnp.float32),
            jax.ShapeDtypeStruct((piece, width), jnp.float32),
            jax.ShapeDtypeStruct((1, 1), jnp.float32),
        ),
        in_specs=[vmem] * (1 + len(psi_parts)),
        out_specs=(vmem,) * 3,
        compiler_params=params,
        name="totals",
    )(phi_parts, *psi_parts)
    return (grad_phi, grad_psi, loss.reshape(()))


def solution(mesh):
    nrow, ngoal = mesh.shape["row"], mesh.shape["goal"]
    fine = Mesh(mesh.devices.reshape(nrow // 2, 2, ngoal // 8, 8), ALL)
    return jax.shard_map(
        shards,
        mesh=fine,
        in_specs=(P(ALL, None), P(ALL, None), P(ALL)),
        out_specs=(P(ALL, None), P(ALL, None), P()),
        check_vma=False,
    )
```

```python
import functools
import math

import jax
import jax.numpy as jnp
from jax import lax
from jax.experimental import pallas as pl
from jax.experimental.pallas import tpu as pltpu
from jax.sharding import Mesh, PartitionSpec as P

ALL = ("y", "core", "x", "z")
PEERS = ("y", "core", "x")
PLANE = ("y", "x")
EXTRA = 8
CHUNK = 256
LANES = 128
LOG2E = math.log2(math.e)
SHIFTS = (1, 2, 3, 4, 5, 6, 7)
VMEM_LIMIT = 24 * 1024 * 1024


def nt(left, right):
    return lax.dot_general(
        left, right, (((1,), (1,)), ((), ())), preferred_element_type=jnp.float32
    )


def tn(left, right):
    return lax.dot_general(
        left, right, (((0,), (0,)), ((), ())), preferred_element_type=jnp.float32
    )


def nn(left, right):
    return lax.dot_general(
        left, right, (((1,), (0,)), ((), ())), preferred_element_type=jnp.float32
    )


def to_rows(lanes):
    return jnp.transpose(jnp.broadcast_to(lanes, (LANES, LANES)))


def to_lanes(column):
    return jnp.transpose(jnp.broadcast_to(column, (LANES, LANES)))[0:1]


def place_shards(place_ref, pieces, psi_ref):
    own = place_ref[0]
    shard = pieces[0].shape[0]
    nz = len(pieces)
    for piece, shift in zip(pieces, (0,) + SHIFTS):
        slot = lax.rem(own + nz - shift, nz)
        psi_ref[pl.ds(pl.multiple_of(slot * shard, shard), shard), :] = piece[...]


def row_places(phi_ref, first, shards, shard):
    out = []
    for k in range(shards):
        block = phi_ref[first + k]
        code = to_rows(block[shard : shard + 1, :LANES].astype(jnp.float32))
        out.append(code[:shard] * 256.0 + code[shard : 2 * shard])
    return jnp.concatenate(out, axis=0)


def hit_mask(places, base, ncol):
    rel = places - base
    lane = lax.broadcasted_iota(jnp.int32, rel.shape, 1).astype(jnp.float32)
    off = rel - lane
    return jnp.concatenate(
        [off == float(t * LANES) for t in range(ncol // LANES)], axis=1
    )


def pack_kernel(phi_in, pos_in, out_ref, block_ref, pos_ref, sems, sem):
    shard, width = phi_in.shape
    loads = [
        pltpu.make_async_copy(pos_in, pos_ref, sems.at[0]),
        pltpu.make_async_copy(phi_in, block_ref.at[:shard], sems.at[1]),
    ]
    for load in loads:
        load.start()
    loads[0].wait()
    places = pos_ref[...]
    high = lax.shift_right_logical(places, 8)
    code = jnp.concatenate([high, places - high * 256], axis=1).astype(jnp.float32)
    code = jnp.concatenate([code, jnp.zeros((1, width - 2 * shard), jnp.float32)], axis=1)
    block_ref[shard:, :] = jnp.broadcast_to(code, (EXTRA, width)).astype(jnp.bfloat16)
    loads[1].wait()
    copies = [
        pltpu.make_async_copy(block_ref, out_ref.at[k], sem.at[k])
        for k in range(out_ref.shape[0])
    ]
    for copy in copies:
        copy.start()
    for copy in copies:
        copy.wait()


def chunks_of(refs, shard):
    per = CHUNK // shard
    out = []
    for half, ref in enumerate(refs):
        for first in range(0, ref.shape[0], per):
            out.append((len(out), half, first, ref))
    return out


def line_of(place_ref, number, half, count):
    lines = CHUNK // LANES
    core = place_ref[2]
    whose = core if half == 0 else 1 - core
    return whose * (count // 2 * lines) + (number % (count // 2)) * lines


def row_lines(scale2, shard, phi_ref, psi):
    per = CHUNK // shard
    out = []
    for _, _, first, ref in chunks_of((phi_ref,), shard):
        rows = ref[first : first + per, :shard, :].reshape(CHUNK, -1)
        logits = nt(rows, psi) * scale2
        peak = jnp.max(logits, axis=1, keepdims=True)
        total = jnp.sum(jnp.exp2(logits - peak), axis=1, keepdims=True)
        lse = peak + jnp.log2(total)
        for t in range(CHUNK // LANES):
            out.append(to_lanes(lse[t * LANES : (t + 1) * LANES]))
    return jnp.concatenate(out, axis=0)


def own_rows_kernel(scale2, shard, place_ref, phi_ref, *refs):
    pieces = refs[:-4]
    line_ref, psi_out, psi_ref, sem = refs[-4:]
    place_shards(place_ref, pieces, psi_ref)
    copy = pltpu.make_async_copy(psi_ref, psi_out, sem)
    copy.start()
    line_ref[...] = row_lines(scale2, shard, phi_ref, psi_ref[...])
    copy.wait()


def all_rows_kernel(
    scale2, shard, place_ref, phi_ref, line_ref, psi_ref, row_ref
):
    count = line_ref.shape[0]
    npeer = row_ref.shape[0]
    core = place_ref[2]
    lines = row_lines(scale2, shard, phi_ref, psi_ref[...])
    for whose, part in ((core, line_ref[...]), (1 - core, lines)):
        at = pl.multiple_of(whose * count, count)
        row_ref[:, pl.ds(at, count), :] = jnp.broadcast_to(part[None], (npeer, count, LANES))


def block_copies(pairs, sems):
    out = []
    for k, (src, dst) in enumerate(pairs):
        cuts = [pl.ds(r, CHUNK) for r in range(0, src.shape[0], CHUNK)]
        out.append(
            [
                pltpu.make_async_copy(src.at[cut], dst.at[cut], sems.at[k, i])
                for i, cut in enumerate(cuts)
            ]
        )
    return out


def cols_kernel(
    scale2, shard, place_ref, own_ref, other_ref, psi_in, col_ref, peak_ref, psi_ref, sem
):
    copy = pltpu.make_async_copy(psi_in, psi_ref, sem)
    copy.start()
    nz = col_ref.shape[0]
    ncol = psi_ref.shape[0]
    nline = ncol // LANES
    per = CHUNK // shard
    base = place_ref[1].astype(jnp.float32)
    lane = lax.broadcasted_iota(jnp.int32, (CHUNK, LANES), 1).astype(jnp.float32)
    copy.wait()
    psi = psi_ref[...]
    col_max = jnp.full((1, ncol), -1e30, jnp.float32)
    col_sum = jnp.zeros((1, ncol), jnp.float32)
    count = jnp.zeros((LANES, LANES), jnp.float32)
    hit_sum = jnp.zeros((1, ncol), jnp.float32)
    for _, _, first, phi_ref in chunks_of((own_ref, other_ref), shard):
        rows = phi_ref[first : first + per, :shard, :].reshape(CHUNK, -1)
        logits = nt(rows, psi) * scale2
        new_max = jnp.maximum(col_max, jnp.max(logits, axis=0, keepdims=True))
        part = jnp.sum(jnp.exp2(logits - new_max), axis=0, keepdims=True)
        col_sum = col_sum * jnp.exp2(col_max - new_max) + part
        col_max = new_max
        places = row_places(phi_ref, first, per, shard)
        hit = hit_mask(places, base, ncol)
        hit_sum = hit_sum + jnp.sum(jnp.where(hit, logits, 0.0), axis=0, keepdims=True)
        high = jnp.floor((places - base) * (1.0 / LANES))
        low = places - base - high * LANES
        high = jnp.where(high == lane, 1.0, 0.0).astype(jnp.bfloat16)
        low = jnp.where(low == lane, 1.0, 0.0).astype(jnp.bfloat16)
        count = count + tn(high, low)
    col_lse = col_max + jnp.log2(col_sum)
    for k, line in enumerate((col_lse, hit_sum)):
        for t in range(nline):
            cut = line[:, t * LANES : (t + 1) * LANES]
            at = 2 * k * nline + t
            col_ref[:, at : at + 1, :] = jnp.broadcast_to(cut[None], (nz, 1, LANES))
    for t in range(nline):
        peak_ref[t : t + 1, :] = col_max[:, t * LANES : (t + 1) * LANES]
    col_ref[:, nline : 2 * nline, :] = jnp.broadcast_to(
        count[None, :nline, :], (nz, nline, LANES)
    )


def tail_rows(value, width):
    terms = jnp.broadcast_to(value, (1, width))
    first = terms.astype(jnp.bfloat16).astype(jnp.float32)
    second = (terms - first).astype(jnp.bfloat16).astype(jnp.float32)
    third = terms - first - second
    row = lax.broadcasted_iota(jnp.int32, (EXTRA, width), 0)
    full = jnp.where(
        row == 0, first, jnp.where(row == 1, second, jnp.where(row == 2, third, 0.0))
    )
    return full.astype(jnp.bfloat16)


def probs_kernel(
    scale, scale2, shard, place_ref, own_ref, other_ref, psi_in, rows_ref, others_ref, peak_ref, *refs
):
    prob_out, exp_out, tail_ref, shift_ref, psi_ref, prob_ref, exp_ref, sem, sems = refs
    copy = pltpu.make_async_copy(psi_in, psi_ref, sem)
    copy.start()
    ncol, width = psi_ref.shape
    per = CHUNK // shard
    base = place_ref[1].astype(jnp.float32)
    row_parts = jnp.concatenate([rows_ref[...], others_ref[...]], axis=0)
    row_peak = jnp.max(row_parts, axis=0)
    row_lse = row_peak + jnp.log2(jnp.sum(jnp.exp2(row_parts - row_peak[None]), axis=0))
    tail_ref[...] = tail_rows(jnp.sum(row_lse, keepdims=True), width)
    shift_ref[...] = row_lse - math.log2(scale)
    copy.wait()
    psi = psi_ref[...]
    prob_stores, exp_stores = block_copies([(prob_ref, prob_out), (exp_ref, exp_out)], sems)
    peak = jnp.concatenate([peak_ref[t : t + 1] for t in range(ncol // LANES)], axis=1)
    chunks = chunks_of((own_ref, other_ref), shard)
    for number, half, first, phi_ref in chunks:
        rows = phi_ref[first : first + per, :shard, :].reshape(CHUNK, width)
        logits = nt(rows, psi) * scale2
        at = line_of(place_ref, number, half, len(chunks))
        lse = jnp.concatenate(
            [to_rows(shift_ref[pl.ds(at + t, 1), :]) for t in range(CHUNK // LANES)],
            axis=0,
        )
        lse = jnp.concatenate([lse] * (ncol // LANES), axis=1)
        hit = hit_mask(row_places(phi_ref, first, per, shard), base, ncol)
        prob = jnp.exp2(logits - lse) - jnp.where(hit, 2.0 * scale, 0.0)
        prob_ref[number * CHUNK : (number + 1) * CHUNK, :] = prob.astype(jnp.bfloat16)
        prob_stores[number].start()
        part = jnp.exp2(logits - peak).astype(jnp.bfloat16)
        exp_ref[number * CHUNK : (number + 1) * CHUNK, :] = part
        exp_stores[number].start()
    for store in prob_stores + exp_stores:
        store.wait()


def weights_kernel(scale, shard, cols_ref, peak_ref, psi_in, prob_in, exp_in, *refs):
    gown_ref, gother_ref, w_ref, psi_ref, prob_ref, exp_ref, sem, sems = refs
    copy = pltpu.make_async_copy(psi_in, psi_ref, sem)
    loads = block_copies([(prob_in, prob_ref), (exp_in, exp_ref)], sems)
    loads[0][0].start()
    loads[1][0].start()
    copy.start()
    for pair in zip(loads[0][1:], loads[1][1:]):
        for load in pair:
            load.start()
    ncol, width = psi_ref.shape
    per = CHUNK // shard
    nline = ncol // LANES
    col_parts = cols_ref[:, :nline, :]
    col_peak = jnp.max(col_parts, axis=0)
    col_lse = col_peak + jnp.log2(jnp.sum(jnp.exp2(col_parts - col_peak[None]), axis=0))
    counts = jnp.sum(cols_ref[:, nline : 2 * nline, :], axis=0)
    hits = jnp.sum(cols_ref[:, 2 * nline :, :], axis=0)
    col_total = jnp.sum(counts * col_lse - 2.0 * hits, keepdims=True)
    tail = jnp.broadcast_to(tail_rows(col_total, width)[None], (per, EXTRA, width))
    factor = counts * scale * jnp.exp2(peak_ref[...] - col_lse)
    factor = jnp.concatenate([factor[t : t + 1] for t in range(nline)], axis=1)
    copy.wait()
    psi = psi_ref[...]
    plane = gown_ref.shape[0]
    for number in range(len(loads[0])):
        cut = slice(number * CHUNK, (number + 1) * CHUNK)
        loads[0][number].wait()
        loads[1][number].wait()
        weights = exp_ref[cut, :].astype(jnp.float32) * factor
        weights = (prob_ref[cut, :].astype(jnp.float32) + weights).astype(jnp.bfloat16)
        w_ref[cut, :] = weights
        part = nn(weights, psi).astype(jnp.bfloat16)
        half, first = divmod(number * per, plane)
        out_ref = gother_ref if half else gown_ref
        out_ref[first : first + per, :shard, :] = part.reshape(per, shard, width)
        out_ref[first : first + per, shard:, :] = tail


def join_kernel(shard, own_ref, other_ref, out, out_ref, sems):
    npeer, _, width = own_ref.shape
    copies = []
    for k in range(npeer):
        total = own_ref[k].astype(jnp.float32) + other_ref[k].astype(jnp.float32)
        out_ref[k, :shard, :] = total[:shard].astype(jnp.bfloat16)
        if k == 0:
            loss = jnp.zeros((1, LANES), jnp.float32)
            for r in range(3):
                loss = loss + total[shard + r : shard + r + 1, :LANES]
            tail = tail_rows(loss[:, :1], width)
        out_ref[k, shard:, :] = tail
        if k % 4 == 3:
            cut = pl.ds(k - 3, 4)
            copies.append(
                pltpu.make_async_copy(out_ref.at[cut], out.at[cut], sems.at[k // 4])
            )
            copies[-1].start()
    for copy in copies:
        copy.wait()


def goals_kernel(shard, place_ref, w_ref, own_ref, other_ref, tail_ref, *refs):
    nz = 1 + len(SHIFTS)
    gpsi_refs = refs[:nz]
    (acc_ref,) = refs[nz:]
    nrow, ncol = w_ref.shape
    own = own_ref[:, :shard, :].reshape(nrow // 2, -1)
    other = other_ref[:, :shard, :].reshape(nrow // 2, -1)
    rows = jnp.concatenate([own, other], axis=0)
    for c in range(ncol // CHUNK):
        cut = slice(c * CHUNK, (c + 1) * CHUNK)
        acc_ref[cut, :] = tn(w_ref[:, cut], rows).astype(jnp.bfloat16)
    own = place_ref[0]
    piece = ncol // nz
    for out, shift in zip(gpsi_refs, (0,) + SHIFTS):
        slot = lax.rem(own + shift, nz)
        out[:piece, :] = acc_ref[pl.ds(pl.multiple_of(slot * piece, piece), piece), :]
        out[piece:, :] = tail_ref[...]


def relay_kernel(parity, place_ref, *refs):
    out = refs[-1]
    piece = out.shape[0] - EXTRA
    width = out.shape[1]
    total = refs[0][...].astype(jnp.float32)
    for ref in refs[1:-2]:
        total = total + ref[...].astype(jnp.float32)
    counts = lax.rem(place_ref[0], 2) == parity
    total = total + jnp.where(counts, refs[-2][...].astype(jnp.float32), 0.0)
    out[:piece, :] = total[:piece].astype(jnp.bfloat16)
    loss = jnp.zeros((1, LANES), jnp.float32)
    for r in range(3):
        loss = loss + total[piece + r : piece + r + 1, :LANES]
    out[piece:, :] = tail_rows(loss[:, :1], width)


def total_kernel(nrow, phi_parts_ref, *refs):
    parts = refs[:-3]
    gphi_ref, gpsi_ref, loss_ref = refs[-3:]
    shard = gphi_ref.shape[0]
    piece = gpsi_ref.shape[0]
    total = phi_parts_ref[0].astype(jnp.float32)
    for k in range(1, phi_parts_ref.shape[0]):
        total = total + phi_parts_ref[k].astype(jnp.float32)
    gphi_ref[...] = total[:shard]
    loss = total[shard : shard + 1, :LANES]
    for r in range(1, 3):
        loss = loss + total[shard + r : shard + r + 1, :LANES]
    total = parts[0][...].astype(jnp.float32)
    for part in parts[1:]:
        total = total + part[...].astype(jnp.float32)
    gpsi_ref[...] = total[:piece]
    for r in range(3):
        loss = loss + total[piece + r : piece + r + 1, :LANES]
    loss_ref[...] = loss[:, :1] * (math.log(2.0) / nrow)


def shards(phi, psi, positives):
    shard, width = phi.shape
    piece = psi.shape[0]
    npeer = lax.axis_size(PEERS)
    nz = lax.axis_size("z")
    nrow = npeer * shard
    ncol = nz * piece
    scale = 1.0 / math.sqrt(width)
    scale2 = scale * LOG2E
    peer = lax.axis_index(PEERS)
    place = jnp.stack(
        [lax.axis_index("z"), peer * ncol, lax.axis_index("core")]
    ).astype(jnp.int32)

    def spread(array, axes):
        return lax.all_to_all(array, axes, 0, 0, tiled=True)

    def swap(array):
        return lax.ppermute(array, "core", [(0, 1), (1, 0)])

    def move(array, shift):
        return lax.ppermute(array, "z", [(i, (i + shift) % nz) for i in range(nz)])

    smem = pl.BlockSpec(memory_space=pltpu.SMEM)
    vmem = pl.BlockSpec(memory_space=pltpu.VMEM)
    hbm = pl.BlockSpec(memory_space=pltpu.HBM)
    params = pltpu.CompilerParams(vmem_limit_bytes=VMEM_LIMIT)

    nplane = npeer // 2
    packed = pl.pallas_call(
        pack_kernel,
        out_shape=pltpu.HBM((nplane, shard + EXTRA, width), jnp.bfloat16),
        in_specs=[hbm] * 2,
        out_specs=hbm,
        scratch_shapes=[
            pltpu.VMEM((shard + EXTRA, width), jnp.bfloat16),
            pltpu.VMEM((1, shard), jnp.int32),
            pltpu.SemaphoreType.DMA((2,)),
            pltpu.SemaphoreType.DMA((nplane,)),
        ],
        compiler_params=params,
        name="pack",
    )(
        pltpu.with_memory_space_constraint(phi, pltpu.HBM),
        pltpu.with_memory_space_constraint(positives.reshape(1, shard), pltpu.HBM),
    )
    own = spread(packed, PLANE)
    near = {0: psi, 2: move(psi, 2), 6: move(psi, 6), 1: move(psi, 1), 7: move(psi, 7)}
    even = lax.rem(lax.axis_index("z"), 2) == 0
    across = [(i, (i + (2 if i % 2 == 0 else 6)) % nz) for i in range(nz)]
    near[4] = lax.ppermute(jnp.where(even, near[2], near[6]), "z", across)
    near[3] = move(near[2], 1)
    near[5] = move(near[6], 7)
    tied = lax.optimization_barrier((own, *[near[k] for k in range(nz)]))
    own = tied[0]
    near = dict(enumerate(tied[1:]))
    other = swap(own)
    goals = [near[k] for k in range(nz)]
    flops = 2 * nrow * ncol * width

    def cost(products):
        return pl.CostEstimate(
            flops=int(products * flops), bytes_accessed=4 << 20, transcendentals=int(products * nrow * ncol)
        )

    anywhere = pl.BlockSpec(memory_space=pl.ANY)
    dma = pltpu.SemaphoreType.DMA
    nchunk = nrow // CHUNK
    psi_scratch = pltpu.VMEM((ncol, width), jnp.bfloat16)
    tile = jax.ShapeDtypeStruct((nrow, ncol), jnp.bfloat16)
    tile_hbm = pltpu.HBM((nrow, ncol), jnp.bfloat16)
    tile_scratch = pltpu.VMEM((nrow, ncol), jnp.bfloat16)
    own_lines, psi_all, psi_near = pl.pallas_call(
        functools.partial(own_rows_kernel, scale2, shard),
        out_shape=(
            jax.ShapeDtypeStruct((nrow // LANES // 2, LANES), jnp.float32),
            jax.ShapeDtypeStruct((ncol, width), jnp.bfloat16),
            jax.ShapeDtypeStruct((ncol, width), jnp.bfloat16),
        ),
        in_specs=[smem] + [vmem] * (1 + nz),
        out_specs=(vmem, anywhere, vmem),
        scratch_shapes=[dma],
        compiler_params=params,
        cost_estimate=cost(0.5),
        name="own_rows",
    )(place, own, *goals)
    row_stats = pl.pallas_call(
        functools.partial(all_rows_kernel, scale2, shard),
        out_shape=jax.ShapeDtypeStruct((nplane, nrow // LANES, LANES), jnp.float32),
        in_specs=[smem] + [vmem] * 3,
        out_specs=vmem,
        compiler_params=params,
        cost_estimate=cost(0.5),
        name="all_rows",
    )(place, other, own_lines, psi_near)
    row_parts = spread(row_stats, PLANE)

    col_stats, peaks = pl.pallas_call(
        functools.partial(cols_kernel, scale2, shard),
        out_shape=(
            jax.ShapeDtypeStruct((nz, 3 * ncol // LANES, LANES), jnp.float32),
            jax.ShapeDtypeStruct((ncol // LANES, LANES), jnp.float32),
        ),
        in_specs=[smem] + [vmem] * 2 + [anywhere],
        out_specs=(vmem, vmem),
        scratch_shapes=[psi_scratch, dma],
        compiler_params=params,
        cost_estimate=cost(1),
        name="cols",
    )(place, own, other, psi_all)
    row_parts, col_stats = lax.optimization_barrier((row_parts, col_stats))
    row_others = swap(row_parts)
    col_parts = spread(col_stats, "z")

    probs, exps, tail = pl.pallas_call(
        functools.partial(probs_kernel, scale, scale2, shard),
        out_shape=(tile_hbm, tile_hbm, jax.ShapeDtypeStruct((EXTRA, width), jnp.bfloat16)),
        in_specs=[smem] + [vmem] * 2 + [anywhere] + [vmem] * 3,
        out_specs=(hbm, hbm, vmem),
        scratch_shapes=[
            pltpu.VMEM((nrow // LANES, LANES), jnp.float32),
            psi_scratch,
            tile_scratch,
            tile_scratch,
            dma,
            dma((2, nchunk)),
        ],
        compiler_params=params,
        cost_estimate=cost(1),
        name="probs",
    )(place, own, other, psi_all, row_parts, row_others, peaks)

    half = jax.ShapeDtypeStruct((nplane, shard + EXTRA, width), jnp.bfloat16)
    gown, gother, weights = pl.pallas_call(
        functools.partial(weights_kernel, scale, shard),
        out_shape=(half, half, tile),
        in_specs=[vmem] * 2 + [anywhere, hbm, hbm],
        out_specs=(vmem,) * 3,
        scratch_shapes=[psi_scratch, tile_scratch, tile_scratch, dma, dma((2, nchunk))],
        compiler_params=params,
        cost_estimate=cost(1),
        name="weights",
    )(
        col_parts,
        peaks,
        psi_all,
        pltpu.with_memory_space_constraint(probs, pltpu.HBM),
        pltpu.with_memory_space_constraint(exps, pltpu.HBM),
    )
    part = jax.ShapeDtypeStruct((piece + EXTRA, width), jnp.bfloat16)
    gpsi = pl.pallas_call(
        functools.partial(goals_kernel, shard),
        out_shape=(part,) * nz,
        in_specs=[smem] + [vmem] * 4,
        out_specs=(vmem,) * nz,
        scratch_shapes=[pltpu.VMEM((ncol, width), jnp.bfloat16)],
        compiler_params=params,
        cost_estimate=cost(1),
        name="goals",
    )(place, weights, own, other, tail)

    other_part, *gpsi = lax.optimization_barrier((swap(gother), *gpsi))
    joined = pl.pallas_call(
        functools.partial(join_kernel, shard),
        out_shape=pltpu.HBM(half.shape, half.dtype),
        in_specs=[vmem] * 2,
        out_specs=hbm,
        scratch_shapes=[pltpu.VMEM(half.shape, half.dtype), dma((nplane // 4,))],
        compiler_params=params,
        name="join",
    )(gown, other_part)
    phi_parts = spread(joined, PLANE)

    def relay(parity, *parts):
        return pl.pallas_call(
            functools.partial(relay_kernel, parity),
            out_shape=part,
            in_specs=[smem] + [vmem] * len(parts),
            out_specs=vmem,
            compiler_params=params,
            name="relay",
        )(place, *parts)

    over4 = lax.ppermute(gpsi[4], "z", across)
    over3, over5 = move(gpsi[3], 1), move(gpsi[5], 7)
    psi_parts = [gpsi[0], move(gpsi[1], 1), move(gpsi[7], 7)]
    psi_parts.append(move(relay(0, gpsi[2], over3, over4), 2))
    psi_parts.append(move(relay(1, gpsi[6], over5, over4), 6))

    grad_phi, grad_psi, loss = pl.pallas_call(
        functools.partial(total_kernel, nrow * nz),
        out_shape=(
            jax.ShapeDtypeStruct((shard, width), jnp.float32),
            jax.ShapeDtypeStruct((piece, width), jnp.float32),
            jax.ShapeDtypeStruct((1, 1), jnp.float32),
        ),
        in_specs=[vmem] * (1 + len(psi_parts)),
        out_specs=(vmem,) * 3,
        compiler_params=params,
        name="totals",
    )(phi_parts, *psi_parts)
    return (grad_phi, grad_psi, loss.reshape(()))


def solution(mesh):
    nrow, ngoal = mesh.shape["row"], mesh.shape["goal"]
    fine = Mesh(mesh.devices.reshape(nrow // 2, 2, ngoal // 8, 8), ALL)
    return jax.shard_map(
        shards,
        mesh=fine,
        in_specs=(P(ALL, None), P(ALL, None), P(ALL)),
        out_specs=(P(ALL, None), P(ALL, None), P()),
        check_vma=False,
    )
```

```python
import functools
import math

import jax
import jax.numpy as jnp
from jax import lax
from jax.experimental import pallas as pl
from jax.experimental.pallas import tpu as pltpu
from jax.sharding import Mesh, PartitionSpec as P

ALL = ("y", "core", "x", "z")
PEERS = ("y", "core", "x")
PLANE = ("y", "x")
EXTRA = 8
GROUP = 16
CHUNK = 256
LANES = 128
LOG2E = math.log2(math.e)
SHIFTS = (1, 2, 3, 4, 5, 6, 7)
VMEM_LIMIT = 24 * 1024 * 1024


def nt(left, right):
    return lax.dot_general(
        left, right, (((1,), (1,)), ((), ())), preferred_element_type=jnp.float32
    )


def tn(left, right):
    return lax.dot_general(
        left, right, (((0,), (0,)), ((), ())), preferred_element_type=jnp.float32
    )


def nn(left, right):
    return lax.dot_general(
        left, right, (((1,), (0,)), ((), ())), preferred_element_type=jnp.float32
    )


def to_rows(lanes):
    return jnp.transpose(jnp.broadcast_to(lanes, (LANES, LANES)))


def to_lanes(column):
    return jnp.transpose(jnp.broadcast_to(column, (LANES, LANES)))[0:1]


def place_shards(place_ref, pieces, psi_ref):
    own = place_ref[0]
    shard = pieces[0].shape[0]
    nz = len(pieces)
    for piece, shift in zip(pieces, (0,) + SHIFTS):
        slot = lax.rem(own + nz - shift, nz)
        psi_ref[pl.ds(pl.multiple_of(slot * shard, shard), shard), :] = piece[...]


def row_places(phi_ref, first, shards, shard):
    out = []
    for k in range(shards):
        block = phi_ref[first + k]
        code = to_rows(block[shard : shard + 1, :LANES].astype(jnp.float32))
        out.append(code[:shard] * 256.0 + code[shard : 2 * shard])
    return jnp.concatenate(out, axis=0)


def hit_mask(places, base, ncol):
    rel = places - base
    lane = lax.broadcasted_iota(jnp.int32, rel.shape, 1).astype(jnp.float32)
    off = rel - lane
    return jnp.concatenate(
        [off == float(t * LANES) for t in range(ncol // LANES)], axis=1
    )


def pack_kernel(phi_in, pos_in, out_ref, block_ref, pos_ref, sems, sem):
    shard, width = phi_in.shape
    loads = [
        pltpu.make_async_copy(pos_in, pos_ref, sems.at[0]),
        pltpu.make_async_copy(phi_in, block_ref.at[:shard], sems.at[1]),
    ]
    for load in loads:
        load.start()
    loads[0].wait()
    places = pos_ref[...]
    high = lax.shift_right_logical(places, 8)
    code = jnp.concatenate([high, places - high * 256], axis=1).astype(jnp.float32)
    code = jnp.concatenate([code, jnp.zeros((1, width - 2 * shard), jnp.float32)], axis=1)
    block_ref[shard:, :] = jnp.broadcast_to(code, (EXTRA, width)).astype(jnp.bfloat16)
    loads[1].wait()
    copies = [
        pltpu.make_async_copy(block_ref, out_ref.at[k], sem.at[k])
        for k in range(out_ref.shape[0])
    ]
    for copy in copies:
        copy.start()
    for copy in copies:
        copy.wait()


def chunks_of(refs, shard):
    per = CHUNK // shard
    out = []
    for half, ref in enumerate(refs):
        for first in range(0, ref.shape[0], per):
            out.append((len(out), half, first, ref))
    return out


def line_of(place_ref, number, half, count):
    lines = CHUNK // LANES
    core = place_ref[2]
    whose = core if half == 0 else 1 - core
    return whose * (count // 2 * lines) + (number % (count // 2)) * lines


def row_lines(scale2, shard, phi_ref, psi):
    per = CHUNK // shard
    out = []
    for _, _, first, ref in chunks_of((phi_ref,), shard):
        rows = ref[first : first + per, :shard, :].reshape(CHUNK, -1)
        logits = nt(rows, psi) * scale2
        peak = jnp.max(logits, axis=1, keepdims=True)
        total = jnp.sum(jnp.exp2(logits - peak), axis=1, keepdims=True)
        lse = peak + jnp.log2(total)
        for t in range(CHUNK // LANES):
            out.append(to_lanes(lse[t * LANES : (t + 1) * LANES]))
    return jnp.concatenate(out, axis=0)


def own_rows_kernel(scale2, shard, place_ref, phi_ref, *refs):
    pieces = refs[:-4]
    line_ref, psi_out, psi_ref, sem = refs[-4:]
    place_shards(place_ref, pieces, psi_ref)
    copy = pltpu.make_async_copy(psi_ref, psi_out, sem)
    copy.start()
    line_ref[...] = row_lines(scale2, shard, phi_ref, psi_ref[...])
    copy.wait()


def all_rows_kernel(
    scale2, shard, place_ref, phi_ref, line_ref, psi_ref, row_ref
):
    count = line_ref.shape[0]
    npeer = row_ref.shape[0]
    core = place_ref[2]
    lines = row_lines(scale2, shard, phi_ref, psi_ref[...])
    for whose, part in ((core, line_ref[...]), (1 - core, lines)):
        at = pl.multiple_of(whose * count, count)
        row_ref[:, pl.ds(at, count), :] = jnp.broadcast_to(part[None], (npeer, count, LANES))


def cols_kernel(
    scale2, shard, place_ref, own_ref, other_ref, psi_in, col_ref, psi_ref, sem
):
    copy = pltpu.make_async_copy(psi_in, psi_ref, sem)
    copy.start()
    nz = col_ref.shape[0]
    ncol = psi_ref.shape[0]
    nline = ncol // LANES
    per = CHUNK // shard
    base = place_ref[1].astype(jnp.float32)
    lane = lax.broadcasted_iota(jnp.int32, (CHUNK, LANES), 1).astype(jnp.float32)
    copy.wait()
    psi = psi_ref[...]
    col_max = jnp.full((1, ncol), -1e30, jnp.float32)
    col_sum = jnp.zeros((1, ncol), jnp.float32)
    count = jnp.zeros((LANES, LANES), jnp.float32)
    hit_sum = jnp.zeros((1, ncol), jnp.float32)
    for _, _, first, phi_ref in chunks_of((own_ref, other_ref), shard):
        rows = phi_ref[first : first + per, :shard, :].reshape(CHUNK, -1)
        logits = nt(rows, psi) * scale2
        new_max = jnp.maximum(col_max, jnp.max(logits, axis=0, keepdims=True))
        part = jnp.sum(jnp.exp2(logits - new_max), axis=0, keepdims=True)
        col_sum = col_sum * jnp.exp2(col_max - new_max) + part
        col_max = new_max
        places = row_places(phi_ref, first, per, shard)
        hit = hit_mask(places, base, ncol)
        hit_sum = hit_sum + jnp.sum(jnp.where(hit, logits, 0.0), axis=0, keepdims=True)
        high = jnp.floor((places - base) * (1.0 / LANES))
        low = places - base - high * LANES
        high = jnp.where(high == lane, 1.0, 0.0).astype(jnp.bfloat16)
        low = jnp.where(low == lane, 1.0, 0.0).astype(jnp.bfloat16)
        count = count + tn(high, low)
    col_lse = col_max + jnp.log2(col_sum)
    for k, line in enumerate((col_lse, hit_sum)):
        for t in range(nline):
            cut = line[:, t * LANES : (t + 1) * LANES]
            at = 2 * k * nline + t
            col_ref[:, at : at + 1, :] = jnp.broadcast_to(cut[None], (nz, 1, LANES))
    col_ref[:, nline : 2 * nline, :] = jnp.broadcast_to(
        count[None, :nline, :], (nz, nline, LANES)
    )


def tail_rows(value, width):
    terms = jnp.broadcast_to(value, (1, width))
    first = terms.astype(jnp.bfloat16).astype(jnp.float32)
    second = (terms - first).astype(jnp.bfloat16).astype(jnp.float32)
    third = terms - first - second
    row = lax.broadcasted_iota(jnp.int32, (EXTRA, width), 0)
    full = jnp.where(
        row == 0, first, jnp.where(row == 1, second, jnp.where(row == 2, third, 0.0))
    )
    return full.astype(jnp.bfloat16)


def weights_kernel(
    scale, scale2, shard, place_ref, own_ref, other_ref, psi_in, rows_ref, others_ref, *refs
):
    cols_ref, gown_ref, gother_ref, w_ref, tail_ref, shift_ref, psi_ref, sem = refs
    copy = pltpu.make_async_copy(psi_in, psi_ref, sem)
    copy.start()
    ncol, width = psi_ref.shape
    plane = gown_ref.shape[0]
    per = CHUNK // shard
    nline = ncol // LANES
    base = place_ref[1].astype(jnp.float32)
    shift2 = math.log2(scale)

    row_parts = jnp.concatenate([rows_ref[...], others_ref[...]], axis=0)
    row_peak = jnp.max(row_parts, axis=0)
    row_lse = row_peak + jnp.log2(jnp.sum(jnp.exp2(row_parts - row_peak[None]), axis=0))
    tail_ref[...] = tail_rows(jnp.sum(row_lse, keepdims=True), width)
    shift_ref[...] = row_lse - shift2

    col_parts = cols_ref[:, :nline, :]
    col_peak = jnp.max(col_parts, axis=0)
    col_lse = col_peak + jnp.log2(jnp.sum(jnp.exp2(col_parts - col_peak[None]), axis=0))
    counts = jnp.sum(cols_ref[:, nline : 2 * nline, :], axis=0)
    hits = jnp.sum(cols_ref[:, 2 * nline :, :], axis=0)
    col_total = jnp.sum(counts * col_lse - 2.0 * hits, keepdims=True)
    tail = jnp.broadcast_to(tail_rows(col_total, width)[None], (plane, EXTRA, width))
    line = col_lse - jnp.log2(counts) - shift2
    line = jnp.concatenate([line[t : t + 1] for t in range(nline)], axis=1)

    copy.wait()
    psi = psi_ref[...]
    chunks = chunks_of((own_ref, other_ref), shard)
    for number, half, first, phi_ref in chunks:
        rows = phi_ref[first : first + per, :shard, :].reshape(CHUNK, width)
        logits = nt(rows, psi) * scale2
        at = line_of(place_ref, number, half, len(chunks))
        lse = jnp.concatenate(
            [to_rows(shift_ref[pl.ds(at + t, 1), :]) for t in range(CHUNK // LANES)],
            axis=0,
        )
        lse = jnp.concatenate([lse] * nline, axis=1)
        hit = hit_mask(row_places(phi_ref, first, per, shard), base, ncol)
        weights = jnp.exp2(logits - lse) + jnp.exp2(logits - line)
        weights = (weights - jnp.where(hit, 2.0 * scale, 0.0)).astype(jnp.bfloat16)
        w_ref[number * CHUNK : (number + 1) * CHUNK, :] = weights
        out_ref = gother_ref if half else gown_ref
        if (first + per) % GROUP == 0:
            end = (number + 1) * CHUNK
            part = nn(w_ref[end - GROUP * shard : end, :], psi).astype(jnp.bfloat16)
            block = slice(first + per - GROUP, first + per)
            out_ref[block, :shard, :] = part.reshape(GROUP, shard, width)
    gown_ref[:, shard:, :] = tail
    gother_ref[:, shard:, :] = tail


def join_kernel(shard, own_ref, other_ref, out, out_ref, sems):
    npeer, _, width = own_ref.shape
    copies = []
    for k in range(npeer):
        total = own_ref[k].astype(jnp.float32) + other_ref[k].astype(jnp.float32)
        out_ref[k, :shard, :] = total[:shard].astype(jnp.bfloat16)
        if k == 0:
            loss = jnp.zeros((1, LANES), jnp.float32)
            for r in range(3):
                loss = loss + total[shard + r : shard + r + 1, :LANES]
            tail = tail_rows(loss[:, :1], width)
        out_ref[k, shard:, :] = tail
        if k % 4 == 3:
            cut = pl.ds(k - 3, 4)
            copies.append(
                pltpu.make_async_copy(out_ref.at[cut], out.at[cut], sems.at[k // 4])
            )
            copies[-1].start()
    for copy in copies:
        copy.wait()


def goals_kernel(shard, place_ref, w_ref, own_ref, other_ref, tail_ref, *refs):
    nz = 1 + len(SHIFTS)
    gpsi_refs = refs[:nz]
    (acc_ref,) = refs[nz:]
    nrow, ncol = w_ref.shape
    own = own_ref[:, :shard, :].reshape(nrow // 2, -1)
    other = other_ref[:, :shard, :].reshape(nrow // 2, -1)
    rows = jnp.concatenate([own, other], axis=0)
    for c in range(ncol // CHUNK):
        cut = slice(c * CHUNK, (c + 1) * CHUNK)
        acc_ref[cut, :] = tn(w_ref[:, cut], rows).astype(jnp.bfloat16)
    own = place_ref[0]
    piece = ncol // nz
    for out, shift in zip(gpsi_refs, (0,) + SHIFTS):
        slot = lax.rem(own + shift, nz)
        out[:piece, :] = acc_ref[pl.ds(pl.multiple_of(slot * piece, piece), piece), :]
        out[piece:, :] = tail_ref[...]


def relay_kernel(parity, place_ref, *refs):
    out = refs[-1]
    piece = out.shape[0] - EXTRA
    width = out.shape[1]
    total = refs[0][...].astype(jnp.float32)
    for ref in refs[1:-2]:
        total = total + ref[...].astype(jnp.float32)
    counts = lax.rem(place_ref[0], 2) == parity
    total = total + jnp.where(counts, refs[-2][...].astype(jnp.float32), 0.0)
    out[:piece, :] = total[:piece].astype(jnp.bfloat16)
    loss = jnp.zeros((1, LANES), jnp.float32)
    for r in range(3):
        loss = loss + total[piece + r : piece + r + 1, :LANES]
    out[piece:, :] = tail_rows(loss[:, :1], width)


def total_kernel(nrow, phi_parts_ref, *refs):
    parts = refs[:-3]
    gphi_ref, gpsi_ref, loss_ref = refs[-3:]
    shard = gphi_ref.shape[0]
    piece = gpsi_ref.shape[0]
    total = phi_parts_ref[0].astype(jnp.float32)
    for k in range(1, phi_parts_ref.shape[0]):
        total = total + phi_parts_ref[k].astype(jnp.float32)
    gphi_ref[...] = total[:shard]
    loss = total[shard : shard + 1, :LANES]
    for r in range(1, 3):
        loss = loss + total[shard + r : shard + r + 1, :LANES]
    total = parts[0][...].astype(jnp.float32)
    for part in parts[1:]:
        total = total + part[...].astype(jnp.float32)
    gpsi_ref[...] = total[:piece]
    for r in range(3):
        loss = loss + total[piece + r : piece + r + 1, :LANES]
    loss_ref[...] = loss[:, :1] * (math.log(2.0) / nrow)


def shards(phi, psi, positives):
    shard, width = phi.shape
    piece = psi.shape[0]
    npeer = lax.axis_size(PEERS)
    nz = lax.axis_size("z")
    nrow = npeer * shard
    ncol = nz * piece
    scale = 1.0 / math.sqrt(width)
    scale2 = scale * LOG2E
    peer = lax.axis_index(PEERS)
    place = jnp.stack(
        [lax.axis_index("z"), peer * ncol, lax.axis_index("core")]
    ).astype(jnp.int32)

    def spread(array, axes):
        return lax.all_to_all(array, axes, 0, 0, tiled=True)

    def swap(array):
        return lax.ppermute(array, "core", [(0, 1), (1, 0)])

    def move(array, shift):
        return lax.ppermute(array, "z", [(i, (i + shift) % nz) for i in range(nz)])

    smem = pl.BlockSpec(memory_space=pltpu.SMEM)
    vmem = pl.BlockSpec(memory_space=pltpu.VMEM)
    hbm = pl.BlockSpec(memory_space=pltpu.HBM)
    params = pltpu.CompilerParams(vmem_limit_bytes=VMEM_LIMIT)

    nplane = npeer // 2
    packed = pl.pallas_call(
        pack_kernel,
        out_shape=pltpu.HBM((nplane, shard + EXTRA, width), jnp.bfloat16),
        in_specs=[hbm] * 2,
        out_specs=hbm,
        scratch_shapes=[
            pltpu.VMEM((shard + EXTRA, width), jnp.bfloat16),
            pltpu.VMEM((1, shard), jnp.int32),
            pltpu.SemaphoreType.DMA((2,)),
            pltpu.SemaphoreType.DMA((nplane,)),
        ],
        compiler_params=params,
        name="pack",
    )(
        pltpu.with_memory_space_constraint(phi, pltpu.HBM),
        pltpu.with_memory_space_constraint(positives.reshape(1, shard), pltpu.HBM),
    )
    own = spread(packed, PLANE)
    near = {0: psi, 2: move(psi, 2), 6: move(psi, 6), 1: move(psi, 1), 7: move(psi, 7)}
    even = lax.rem(lax.axis_index("z"), 2) == 0
    across = [(i, (i + (2 if i % 2 == 0 else 6)) % nz) for i in range(nz)]
    near[4] = lax.ppermute(jnp.where(even, near[2], near[6]), "z", across)
    near[3] = move(near[2], 1)
    near[5] = move(near[6], 7)
    tied = lax.optimization_barrier((own, *[near[k] for k in range(nz)]))
    own = tied[0]
    near = dict(enumerate(tied[1:]))
    other = swap(own)
    goals = [near[k] for k in range(nz)]
    flops = 2 * nrow * ncol * width

    def cost(products):
        return pl.CostEstimate(
            flops=int(products * flops), bytes_accessed=4 << 20, transcendentals=int(products * nrow * ncol)
        )

    dma = pltpu.SemaphoreType.DMA
    psi_scratch = pltpu.VMEM((ncol, width), jnp.bfloat16)
    tile = jax.ShapeDtypeStruct((nrow, ncol), jnp.bfloat16)
    own_lines, psi_all, psi_near = pl.pallas_call(
        functools.partial(own_rows_kernel, scale2, shard),
        out_shape=(
            jax.ShapeDtypeStruct((nrow // LANES // 2, LANES), jnp.float32),
            pltpu.HBM((ncol, width), jnp.bfloat16),
            jax.ShapeDtypeStruct((ncol, width), jnp.bfloat16),
        ),
        in_specs=[smem] + [vmem] * (1 + nz),
        out_specs=(vmem, hbm, vmem),
        scratch_shapes=[dma],
        compiler_params=params,
        cost_estimate=cost(0.5),
        name="own_rows",
    )(place, own, *goals)
    psi_all = pltpu.with_memory_space_constraint(psi_all, pltpu.HBM)
    row_stats = pl.pallas_call(
        functools.partial(all_rows_kernel, scale2, shard),
        out_shape=jax.ShapeDtypeStruct((nplane, nrow // LANES, LANES), jnp.float32),
        in_specs=[smem] + [vmem] * 3,
        out_specs=vmem,
        compiler_params=params,
        cost_estimate=cost(0.5),
        name="all_rows",
    )(place, other, own_lines, psi_near)
    row_parts = spread(row_stats, PLANE)

    col_stats = pl.pallas_call(
        functools.partial(cols_kernel, scale2, shard),
        out_shape=jax.ShapeDtypeStruct((nz, 3 * ncol // LANES, LANES), jnp.float32),
        in_specs=[smem] + [vmem] * 2 + [hbm],
        out_specs=vmem,
        scratch_shapes=[psi_scratch, dma],
        compiler_params=params,
        cost_estimate=cost(1),
        name="cols",
    )(place, own, other, psi_all)
    row_parts, col_stats = lax.optimization_barrier((row_parts, col_stats))
    row_others = swap(row_parts)
    col_parts = spread(col_stats, "z")

    half = jax.ShapeDtypeStruct((nplane, shard + EXTRA, width), jnp.bfloat16)
    gown, gother, weights, tail = pl.pallas_call(
        functools.partial(weights_kernel, scale, scale2, shard),
        out_shape=(half, half, tile, jax.ShapeDtypeStruct((EXTRA, width), jnp.bfloat16)),
        in_specs=[smem] + [vmem] * 2 + [hbm] + [vmem] * 3,
        out_specs=(vmem,) * 4,
        scratch_shapes=[pltpu.VMEM((nrow // LANES, LANES), jnp.float32), psi_scratch, dma],
        compiler_params=params,
        cost_estimate=cost(2),
        name="weights",
    )(place, own, other, psi_all, row_parts, row_others, col_parts)
    part = jax.ShapeDtypeStruct((piece + EXTRA, width), jnp.bfloat16)
    gpsi = pl.pallas_call(
        functools.partial(goals_kernel, shard),
        out_shape=(part,) * nz,
        in_specs=[smem] + [vmem] * 4,
        out_specs=(vmem,) * nz,
        scratch_shapes=[pltpu.VMEM((ncol, width), jnp.bfloat16)],
        compiler_params=params,
        cost_estimate=cost(1),
        name="goals",
    )(place, weights, own, other, tail)

    other_part, *gpsi = lax.optimization_barrier((swap(gother), *gpsi))
    joined = pl.pallas_call(
        functools.partial(join_kernel, shard),
        out_shape=pltpu.HBM(half.shape, half.dtype),
        in_specs=[vmem] * 2,
        out_specs=hbm,
        scratch_shapes=[pltpu.VMEM(half.shape, half.dtype), dma((nplane // 4,))],
        compiler_params=params,
        name="join",
    )(gown, other_part)
    phi_parts = spread(joined, PLANE)

    def relay(parity, *parts):
        return pl.pallas_call(
            functools.partial(relay_kernel, parity),
            out_shape=part,
            in_specs=[smem] + [vmem] * len(parts),
            out_specs=vmem,
            compiler_params=params,
            name="relay",
        )(place, *parts)

    over4 = lax.ppermute(gpsi[4], "z", across)
    over3, over5 = move(gpsi[3], 1), move(gpsi[5], 7)
    psi_parts = [gpsi[0], move(gpsi[1], 1), move(gpsi[7], 7)]
    psi_parts.append(move(relay(0, gpsi[2], over3, over4), 2))
    psi_parts.append(move(relay(1, gpsi[6], over5, over4), 6))

    grad_phi, grad_psi, loss = pl.pallas_call(
        functools.partial(total_kernel, nrow * nz),
        out_shape=(
            jax.ShapeDtypeStruct((shard, width), jnp.float32),
            jax.ShapeDtypeStruct((piece, width), jnp.float32),
            jax.ShapeDtypeStruct((1, 1), jnp.float32),
        ),
        in_specs=[vmem] * (1 + len(psi_parts)),
        out_specs=(vmem,) * 3,
        compiler_params=params,
        name="totals",
    )(phi_parts, *psi_parts)
    return (grad_phi, grad_psi, loss.reshape(()))


def solution(mesh):
    nrow, ngoal = mesh.shape["row"], mesh.shape["goal"]
    fine = Mesh(mesh.devices.reshape(nrow // 2, 2, ngoal // 8, 8), ALL)
    return jax.shard_map(
        shards,
        mesh=fine,
        in_specs=(P(ALL, None), P(ALL, None), P(ALL)),
        out_specs=(P(ALL, None), P(ALL, None), P()),
        check_vma=False,
    )
```

```python
import functools
import math

import jax
import jax.numpy as jnp
from jax import lax
from jax.experimental import pallas as pl
from jax.experimental.pallas import tpu as pltpu
from jax.sharding import Mesh, PartitionSpec as P

ALL = ("y", "core", "x", "z")
PEERS = ("y", "core", "x")
PLANE = ("y", "x")
EXTRA = 8
GROUP = 16
CHUNK = 256
LANES = 128
LOG2E = math.log2(math.e)
SHIFTS = (1, 2, 3, 4, 5, 6, 7)
VMEM_LIMIT = 24 * 1024 * 1024


def nt(left, right):
    return lax.dot_general(
        left, right, (((1,), (1,)), ((), ())), preferred_element_type=jnp.float32
    )


def tn(left, right):
    return lax.dot_general(
        left, right, (((0,), (0,)), ((), ())), preferred_element_type=jnp.float32
    )


def nn(left, right):
    return lax.dot_general(
        left, right, (((1,), (0,)), ((), ())), preferred_element_type=jnp.float32
    )


def to_rows(lanes):
    return jnp.transpose(jnp.broadcast_to(lanes, (LANES, LANES)))


def to_lanes(column):
    return jnp.transpose(jnp.broadcast_to(column, (LANES, LANES)))[0:1]


def place_shards(place_ref, pieces, psi_ref):
    own = place_ref[0]
    shard = pieces[0].shape[0]
    nz = len(pieces)
    for piece, shift in zip(pieces, (0,) + SHIFTS):
        slot = lax.rem(own + nz - shift, nz)
        psi_ref[pl.ds(pl.multiple_of(slot * shard, shard), shard), :] = piece[...]


def fold_rows(ref, first, count, shard):
    parts = range((ref.shape[1] - EXTRA) // shard)
    cut = slice(first, first + count)
    parts = [ref[cut, t * shard : (t + 1) * shard, :] for t in parts]
    parts = [part.reshape(count * shard, LANES) for part in parts]
    return jnp.concatenate(parts, axis=1)


def put_rows(ref, first, count, shard, rows):
    for t in range(rows.shape[1] // LANES):
        part = rows[:, t * LANES : (t + 1) * LANES].reshape(count, shard, LANES)
        ref[first : first + count, t * shard : (t + 1) * shard, :] = part


def row_places(phi_ref, first, shards, shard):
    out = []
    for k in range(shards):
        block = phi_ref[first + k]
        last = block.shape[0] - EXTRA
        code = to_rows(block[last : last + 1, :].astype(jnp.float32))
        out.append(code[:shard] * 256.0 + code[shard : 2 * shard])
    return jnp.concatenate(out, axis=0)


def hit_mask(places, base, ncol):
    rel = places - base
    lane = lax.broadcasted_iota(jnp.int32, rel.shape, 1).astype(jnp.float32)
    off = rel - lane
    return jnp.concatenate(
        [off == float(t * LANES) for t in range(ncol // LANES)], axis=1
    )


def pack_kernel(phi_in, pos_in, out_ref, block_ref, pos_ref, sems, sem):
    shard, width = phi_in.shape
    loads = [pltpu.make_async_copy(pos_in, pos_ref, sems.at[0])]
    for t in range(width // LANES):
        part = phi_in.at[:, t * LANES : (t + 1) * LANES]
        held = block_ref.at[t * shard : (t + 1) * shard]
        loads.append(pltpu.make_async_copy(part, held, sems.at[1 + t]))
    for load in loads:
        load.start()
    loads[0].wait()
    places = pos_ref[...]
    high = lax.shift_right_logical(places, 8)
    code = jnp.concatenate([high, places - high * 256], axis=1).astype(jnp.float32)
    last = block_ref.shape[0] - EXTRA
    block_ref[last:, :] = jnp.broadcast_to(code, (EXTRA, LANES)).astype(jnp.bfloat16)
    for load in loads[1:]:
        load.wait()
    copies = [
        pltpu.make_async_copy(block_ref, out_ref.at[k], sem.at[k])
        for k in range(out_ref.shape[0])
    ]
    for copy in copies:
        copy.start()
    for copy in copies:
        copy.wait()


def chunks_of(refs, shard):
    per = CHUNK // shard
    out = []
    for half, ref in enumerate(refs):
        for first in range(0, ref.shape[0], per):
            out.append((len(out), half, first, ref))
    return out


def line_of(place_ref, number, half, count):
    lines = CHUNK // LANES
    core = place_ref[2]
    whose = core if half == 0 else 1 - core
    return whose * (count // 2 * lines) + (number % (count // 2)) * lines


def row_lines(scale2, shard, phi_ref, psi):
    per = CHUNK // shard
    out = []
    for _, _, first, ref in chunks_of((phi_ref,), shard):
        rows = fold_rows(ref, first, per, shard)
        logits = nt(rows, psi) * scale2
        peak = jnp.max(logits, axis=1, keepdims=True)
        total = jnp.sum(jnp.exp2(logits - peak), axis=1, keepdims=True)
        lse = peak + jnp.log2(total)
        for t in range(CHUNK // LANES):
            out.append(to_lanes(lse[t * LANES : (t + 1) * LANES]))
    return jnp.concatenate(out, axis=0)


def own_rows_kernel(scale2, shard, place_ref, phi_ref, *refs):
    pieces = refs[:-4]
    line_ref, psi_out, psi_ref, sem = refs[-4:]
    place_shards(place_ref, pieces, psi_ref)
    copy = pltpu.make_async_copy(psi_ref, psi_out, sem)
    copy.start()
    line_ref[...] = row_lines(scale2, shard, phi_ref, psi_ref[...])
    copy.wait()


def all_rows_kernel(
    scale2, shard, place_ref, phi_ref, line_ref, psi_ref, row_ref
):
    count = line_ref.shape[0]
    npeer = row_ref.shape[0]
    core = place_ref[2]
    lines = row_lines(scale2, shard, phi_ref, psi_ref[...])
    for whose, part in ((core, line_ref[...]), (1 - core, lines)):
        at = pl.multiple_of(whose * count, count)
        row_ref[:, pl.ds(at, count), :] = jnp.broadcast_to(part[None], (npeer, count, LANES))


def cols_kernel(
    scale2, shard, place_ref, own_ref, other_ref, psi_in, col_ref, psi_ref, sem
):
    copy = pltpu.make_async_copy(psi_in, psi_ref, sem)
    copy.start()
    nz = col_ref.shape[0]
    ncol = psi_ref.shape[0]
    nline = ncol // LANES
    per = CHUNK // shard
    base = place_ref[1].astype(jnp.float32)
    lane = lax.broadcasted_iota(jnp.int32, (CHUNK, LANES), 1).astype(jnp.float32)
    copy.wait()
    psi = psi_ref[...]
    col_max = jnp.full((1, ncol), -1e30, jnp.float32)
    col_sum = jnp.zeros((1, ncol), jnp.float32)
    count = jnp.zeros((LANES, LANES), jnp.float32)
    hit_sum = jnp.zeros((1, ncol), jnp.float32)
    for _, _, first, phi_ref in chunks_of((own_ref, other_ref), shard):
        rows = fold_rows(phi_ref, first, per, shard)
        logits = nt(rows, psi) * scale2
        new_max = jnp.maximum(col_max, jnp.max(logits, axis=0, keepdims=True))
        part = jnp.sum(jnp.exp2(logits - new_max), axis=0, keepdims=True)
        col_sum = col_sum * jnp.exp2(col_max - new_max) + part
        col_max = new_max
        places = row_places(phi_ref, first, per, shard)
        hit = hit_mask(places, base, ncol)
        hit_sum = hit_sum + jnp.sum(jnp.where(hit, logits, 0.0), axis=0, keepdims=True)
        high = jnp.floor((places - base) * (1.0 / LANES))
        low = places - base - high * LANES
        high = jnp.where(high == lane, 1.0, 0.0).astype(jnp.bfloat16)
        low = jnp.where(low == lane, 1.0, 0.0).astype(jnp.bfloat16)
        count = count + tn(high, low)
    col_lse = col_max + jnp.log2(col_sum)
    for k, line in enumerate((col_lse, hit_sum)):
        for t in range(nline):
            cut = line[:, t * LANES : (t + 1) * LANES]
            at = 2 * k * nline + t
            col_ref[:, at : at + 1, :] = jnp.broadcast_to(cut[None], (nz, 1, LANES))
    col_ref[:, nline : 2 * nline, :] = jnp.broadcast_to(
        count[None, :nline, :], (nz, nline, LANES)
    )


def tail_rows(value, width):
    terms = jnp.broadcast_to(value, (1, width))
    first = terms.astype(jnp.bfloat16).astype(jnp.float32)
    second = (terms - first).astype(jnp.bfloat16).astype(jnp.float32)
    third = terms - first - second
    row = lax.broadcasted_iota(jnp.int32, (EXTRA, width), 0)
    full = jnp.where(
        row == 0, first, jnp.where(row == 1, second, jnp.where(row == 2, third, 0.0))
    )
    return full.astype(jnp.bfloat16)


def weights_kernel(
    scale, scale2, shard, place_ref, own_ref, other_ref, psi_in, rows_ref, others_ref, *refs
):
    cols_ref, gown_ref, gother_ref, w_ref, tail_ref, shift_ref, psi_ref, sem = refs
    copy = pltpu.make_async_copy(psi_in, psi_ref, sem)
    copy.start()
    ncol, width = psi_ref.shape
    plane = gown_ref.shape[0]
    per = CHUNK // shard
    nline = ncol // LANES
    base = place_ref[1].astype(jnp.float32)
    shift2 = math.log2(scale)

    row_parts = jnp.concatenate([rows_ref[...], others_ref[...]], axis=0)
    row_peak = jnp.max(row_parts, axis=0)
    row_lse = row_peak + jnp.log2(jnp.sum(jnp.exp2(row_parts - row_peak[None]), axis=0))
    tail_ref[...] = tail_rows(jnp.sum(row_lse, keepdims=True), LANES)
    shift_ref[...] = row_lse - shift2

    col_parts = cols_ref[:, :nline, :]
    col_peak = jnp.max(col_parts, axis=0)
    col_lse = col_peak + jnp.log2(jnp.sum(jnp.exp2(col_parts - col_peak[None]), axis=0))
    counts = jnp.sum(cols_ref[:, nline : 2 * nline, :], axis=0)
    hits = jnp.sum(cols_ref[:, 2 * nline :, :], axis=0)
    col_total = jnp.sum(counts * col_lse - 2.0 * hits, keepdims=True)
    last = gown_ref.shape[1] - EXTRA
    tail = jnp.broadcast_to(tail_rows(col_total, LANES)[None], (plane, EXTRA, LANES))
    line = col_lse - jnp.log2(counts) - shift2
    line = jnp.concatenate([line[t : t + 1] for t in range(nline)], axis=1)

    copy.wait()
    psi = psi_ref[...]
    chunks = chunks_of((own_ref, other_ref), shard)
    for number, half, first, phi_ref in chunks:
        rows = fold_rows(phi_ref, first, per, shard)
        logits = nt(rows, psi) * scale2
        at = line_of(place_ref, number, half, len(chunks))
        lse = jnp.concatenate(
            [to_rows(shift_ref[pl.ds(at + t, 1), :]) for t in range(CHUNK // LANES)],
            axis=0,
        )
        lse = jnp.concatenate([lse] * nline, axis=1)
        hit = hit_mask(row_places(phi_ref, first, per, shard), base, ncol)
        weights = jnp.exp2(logits - lse) + jnp.exp2(logits - line)
        weights = (weights - jnp.where(hit, 2.0 * scale, 0.0)).astype(jnp.bfloat16)
        w_ref[number * CHUNK : (number + 1) * CHUNK, :] = weights
        out_ref = gother_ref if half else gown_ref
        if (first + per) % GROUP == 0:
            end = (number + 1) * CHUNK
            part = nn(w_ref[end - GROUP * shard : end, :], psi).astype(jnp.bfloat16)
            put_rows(out_ref, first + per - GROUP, GROUP, shard, part)
    gown_ref[:, last:, :] = tail
    gother_ref[:, last:, :] = tail


def join_kernel(own_ref, other_ref, out, out_ref, sems):
    npeer = own_ref.shape[0]
    last = own_ref.shape[1] - EXTRA
    copies = []
    for k in range(npeer):
        total = own_ref[k].astype(jnp.float32) + other_ref[k].astype(jnp.float32)
        out_ref[k, :last, :] = total[:last].astype(jnp.bfloat16)
        if k == 0:
            loss = jnp.zeros((1, LANES), jnp.float32)
            for r in range(3):
                loss = loss + total[last + r : last + r + 1]
            tail = tail_rows(loss[:, :1], LANES)
        out_ref[k, last:, :] = tail
        if k % 4 == 3:
            cut = pl.ds(k - 3, 4)
            copies.append(
                pltpu.make_async_copy(out_ref.at[cut], out.at[cut], sems.at[k // 4])
            )
            copies[-1].start()
    for copy in copies:
        copy.wait()


def goals_kernel(shard, place_ref, w_ref, own_ref, other_ref, tail_ref, *refs):
    nz = 1 + len(SHIFTS)
    gpsi_refs = refs[:nz]
    (acc_ref,) = refs[nz:]
    nrow, ncol = w_ref.shape
    halves = [fold_rows(ref, 0, ref.shape[0], shard) for ref in (own_ref, other_ref)]
    rows = jnp.concatenate(halves, axis=0)
    for c in range(ncol // CHUNK):
        cut = slice(c * CHUNK, (c + 1) * CHUNK)
        acc_ref[cut, :] = tn(w_ref[:, cut], rows).astype(jnp.bfloat16)
    own = place_ref[0]
    piece = ncol // nz
    for out, shift in zip(gpsi_refs, (0,) + SHIFTS):
        slot = lax.rem(own + shift, nz)
        part = acc_ref[pl.ds(pl.multiple_of(slot * piece, piece), piece), :]
        for t in range(part.shape[1] // LANES):
            cut = slice(t * LANES, (t + 1) * LANES)
            out[t * piece : (t + 1) * piece, :] = part[:, cut]
        out[out.shape[0] - EXTRA :, :] = tail_ref[...]


def relay_kernel(parity, place_ref, *refs):
    out = refs[-1]
    piece = out.shape[0] - EXTRA
    width = out.shape[1]
    total = refs[0][...].astype(jnp.float32)
    for ref in refs[1:-2]:
        total = total + ref[...].astype(jnp.float32)
    counts = lax.rem(place_ref[0], 2) == parity
    total = total + jnp.where(counts, refs[-2][...].astype(jnp.float32), 0.0)
    out[:piece, :] = total[:piece].astype(jnp.bfloat16)
    loss = jnp.zeros((1, LANES), jnp.float32)
    for r in range(3):
        loss = loss + total[piece + r : piece + r + 1, :LANES]
    out[piece:, :] = tail_rows(loss[:, :1], width)


def total_kernel(nrow, phi_parts_ref, *refs):
    parts = refs[:-3]
    gphi_ref, gpsi_ref, loss_ref = refs[-3:]
    shard = gphi_ref.shape[0]
    piece = gpsi_ref.shape[0]
    total = phi_parts_ref[0].astype(jnp.float32)
    for k in range(1, phi_parts_ref.shape[0]):
        total = total + phi_parts_ref[k].astype(jnp.float32)
    for t in range(gphi_ref.shape[1] // LANES):
        gphi_ref[:, t * LANES : (t + 1) * LANES] = total[t * shard : (t + 1) * shard]
    last = total.shape[0] - EXTRA
    loss = total[last : last + 1]
    for r in range(1, 3):
        loss = loss + total[last + r : last + r + 1]
    total = parts[0][...].astype(jnp.float32)
    for part in parts[1:]:
        total = total + part[...].astype(jnp.float32)
    for t in range(gpsi_ref.shape[1] // LANES):
        gpsi_ref[:, t * LANES : (t + 1) * LANES] = total[t * piece : (t + 1) * piece]
    last = total.shape[0] - EXTRA
    for r in range(3):
        loss = loss + total[last + r : last + r + 1]
    loss_ref[...] = loss[:, :1] * (math.log(2.0) / nrow)


def shards(phi, psi, positives):
    shard, width = phi.shape
    piece = psi.shape[0]
    npeer = lax.axis_size(PEERS)
    nz = lax.axis_size("z")
    nrow = npeer * shard
    ncol = nz * piece
    scale = 1.0 / math.sqrt(width)
    scale2 = scale * LOG2E
    peer = lax.axis_index(PEERS)
    place = jnp.stack(
        [lax.axis_index("z"), peer * ncol, lax.axis_index("core")]
    ).astype(jnp.int32)

    def spread(array, axes):
        return lax.all_to_all(array, axes, 0, 0, tiled=True)

    def swap(array):
        return lax.ppermute(array, "core", [(0, 1), (1, 0)])

    def move(array, shift):
        return lax.ppermute(array, "z", [(i, (i + shift) % nz) for i in range(nz)])

    smem = pl.BlockSpec(memory_space=pltpu.SMEM)
    vmem = pl.BlockSpec(memory_space=pltpu.VMEM)
    hbm = pl.BlockSpec(memory_space=pltpu.HBM)
    params = pltpu.CompilerParams(vmem_limit_bytes=VMEM_LIMIT)

    nplane = npeer // 2
    fold = shard * width // LANES + EXTRA
    half = jax.ShapeDtypeStruct((nplane, fold, LANES), jnp.bfloat16)
    packed = pl.pallas_call(
        pack_kernel,
        out_shape=pltpu.HBM(half.shape, half.dtype),
        in_specs=[hbm] * 2,
        out_specs=hbm,
        scratch_shapes=[
            pltpu.VMEM(half.shape[1:], half.dtype),
            pltpu.VMEM((1, shard), jnp.int32),
            pltpu.SemaphoreType.DMA((1 + width // LANES,)),
            pltpu.SemaphoreType.DMA((nplane,)),
        ],
        compiler_params=params,
        name="pack",
    )(
        pltpu.with_memory_space_constraint(phi, pltpu.HBM),
        pltpu.with_memory_space_constraint(positives.reshape(1, shard), pltpu.HBM),
    )
    own = spread(packed, PLANE)
    near = {0: psi, 2: move(psi, 2), 6: move(psi, 6), 1: move(psi, 1), 7: move(psi, 7)}
    even = lax.rem(lax.axis_index("z"), 2) == 0
    across = [(i, (i + (2 if i % 2 == 0 else 6)) % nz) for i in range(nz)]
    near[4] = lax.ppermute(jnp.where(even, near[2], near[6]), "z", across)
    near[3] = move(near[2], 1)
    near[5] = move(near[6], 7)
    tied = lax.optimization_barrier((own, *[near[k] for k in range(nz)]))
    own = tied[0]
    near = dict(enumerate(tied[1:]))
    other = swap(own)
    goals = [near[k] for k in range(nz)]
    flops = 2 * nrow * ncol * width

    def cost(products):
        return pl.CostEstimate(
            flops=int(products * flops), bytes_accessed=4 << 20, transcendentals=int(products * nrow * ncol)
        )

    dma = pltpu.SemaphoreType.DMA
    psi_scratch = pltpu.VMEM((ncol, width), jnp.bfloat16)
    tile = jax.ShapeDtypeStruct((nrow, ncol), jnp.bfloat16)
    own_lines, psi_all, psi_near = pl.pallas_call(
        functools.partial(own_rows_kernel, scale2, shard),
        out_shape=(
            jax.ShapeDtypeStruct((nrow // LANES // 2, LANES), jnp.float32),
            pltpu.HBM((ncol, width), jnp.bfloat16),
            jax.ShapeDtypeStruct((ncol, width), jnp.bfloat16),
        ),
        in_specs=[smem] + [vmem] * (1 + nz),
        out_specs=(vmem, hbm, vmem),
        scratch_shapes=[dma],
        compiler_params=params,
        cost_estimate=cost(0.5),
        name="own_rows",
    )(place, own, *goals)
    psi_all = pltpu.with_memory_space_constraint(psi_all, pltpu.HBM)
    row_stats = pl.pallas_call(
        functools.partial(all_rows_kernel, scale2, shard),
        out_shape=jax.ShapeDtypeStruct((nplane, nrow // LANES, LANES), jnp.float32),
        in_specs=[smem] + [vmem] * 3,
        out_specs=vmem,
        compiler_params=params,
        cost_estimate=cost(0.5),
        name="all_rows",
    )(place, other, own_lines, psi_near)
    row_parts = spread(row_stats, PLANE)

    col_stats = pl.pallas_call(
        functools.partial(cols_kernel, scale2, shard),
        out_shape=jax.ShapeDtypeStruct((nz, 3 * ncol // LANES, LANES), jnp.float32),
        in_specs=[smem] + [vmem] * 2 + [hbm],
        out_specs=vmem,
        scratch_shapes=[psi_scratch, dma],
        compiler_params=params,
        cost_estimate=cost(1),
        name="cols",
    )(place, own, other, psi_all)
    row_parts, col_stats = lax.optimization_barrier((row_parts, col_stats))
    row_others = swap(row_parts)
    col_parts = spread(col_stats, "z")

    gown, gother, weights, tail = pl.pallas_call(
        functools.partial(weights_kernel, scale, scale2, shard),
        out_shape=(half, half, tile, jax.ShapeDtypeStruct((EXTRA, LANES), jnp.bfloat16)),
        in_specs=[smem] + [vmem] * 2 + [hbm] + [vmem] * 3,
        out_specs=(vmem,) * 4,
        scratch_shapes=[pltpu.VMEM((nrow // LANES, LANES), jnp.float32), psi_scratch, dma],
        compiler_params=params,
        cost_estimate=cost(2),
        name="weights",
    )(place, own, other, psi_all, row_parts, row_others, col_parts)
    part = jax.ShapeDtypeStruct((piece * width // LANES + EXTRA, LANES), jnp.bfloat16)
    gpsi = pl.pallas_call(
        functools.partial(goals_kernel, shard),
        out_shape=(part,) * nz,
        in_specs=[smem] + [vmem] * 4,
        out_specs=(vmem,) * nz,
        scratch_shapes=[pltpu.VMEM((ncol, width), jnp.bfloat16)],
        compiler_params=params,
        cost_estimate=cost(1),
        name="goals",
    )(place, weights, own, other, tail)

    other_part, *gpsi = lax.optimization_barrier((swap(gother), *gpsi))
    joined = pl.pallas_call(
        join_kernel,
        out_shape=pltpu.HBM(half.shape, half.dtype),
        in_specs=[vmem] * 2,
        out_specs=hbm,
        scratch_shapes=[pltpu.VMEM(half.shape, half.dtype), dma((nplane // 4,))],
        compiler_params=params,
        name="join",
    )(gown, other_part)
    phi_parts = spread(joined, PLANE)

    def relay(parity, *parts):
        return pl.pallas_call(
            functools.partial(relay_kernel, parity),
            out_shape=part,
            in_specs=[smem] + [vmem] * len(parts),
            out_specs=vmem,
            compiler_params=params,
            name="relay",
        )(place, *parts)

    over4 = lax.ppermute(gpsi[4], "z", across)
    over3, over5 = move(gpsi[3], 1), move(gpsi[5], 7)
    psi_parts = [gpsi[0], move(gpsi[1], 1), move(gpsi[7], 7)]
    psi_parts.append(move(relay(0, gpsi[2], over3, over4), 2))
    psi_parts.append(move(relay(1, gpsi[6], over5, over4), 6))

    grad_phi, grad_psi, loss = pl.pallas_call(
        functools.partial(total_kernel, nrow * nz),
        out_shape=(
            jax.ShapeDtypeStruct((shard, width), jnp.float32),
            jax.ShapeDtypeStruct((piece, width), jnp.float32),
            jax.ShapeDtypeStruct((1, 1), jnp.float32),
        ),
        in_specs=[vmem] * (1 + len(psi_parts)),
        out_specs=(vmem,) * 3,
        compiler_params=params,
        name="totals",
    )(phi_parts, *psi_parts)
    return (grad_phi, grad_psi, loss.reshape(()))


def solution(mesh):
    nrow, ngoal = mesh.shape["row"], mesh.shape["goal"]
    fine = Mesh(mesh.devices.reshape(nrow // 2, 2, ngoal // 8, 8), ALL)
    return jax.shard_map(
        shards,
        mesh=fine,
        in_specs=(P(ALL, None), P(ALL, None), P(ALL)),
        out_specs=(P(ALL, None), P(ALL, None), P()),
        check_vma=False,
    )
```

```python
import functools
import math

import jax
import jax.numpy as jnp
from jax import lax
from jax.experimental import pallas as pl
from jax.experimental.pallas import tpu as pltpu
from jax.sharding import Mesh, PartitionSpec as P

ALL = ("y", "core", "x", "z")
PEERS = ("y", "core", "x")
PLANE = ("y", "x")
EXTRA = 8
GROUP = 16
CHUNK = 256
LANES = 128
LOG2E = math.log2(math.e)
SHIFTS = (1, 2, 3, 4, 5, 6, 7)
VMEM_LIMIT = 24 * 1024 * 1024


def nt(left, right):
    return lax.dot_general(
        left, right, (((1,), (1,)), ((), ())), preferred_element_type=jnp.float32
    )


def tn(left, right):
    return lax.dot_general(
        left, right, (((0,), (0,)), ((), ())), preferred_element_type=jnp.float32
    )


def nn(left, right):
    return lax.dot_general(
        left, right, (((1,), (0,)), ((), ())), preferred_element_type=jnp.float32
    )


def to_rows(lanes):
    return jnp.transpose(jnp.broadcast_to(lanes, (LANES, LANES)))


def to_lanes(column):
    return jnp.transpose(jnp.broadcast_to(column, (LANES, LANES)))[0:1]


def place_shards(place_ref, pieces, psi_ref):
    own = place_ref[0]
    shard = pieces[0].shape[0]
    nz = len(pieces)
    for piece, shift in zip(pieces, (0,) + SHIFTS):
        slot = lax.rem(own + nz - shift, nz)
        psi_ref[pl.ds(pl.multiple_of(slot * shard, shard), shard), :] = piece[...]


def fold_rows(ref, first, count, shard):
    parts = range((ref.shape[1] - EXTRA) // shard)
    cut = slice(first, first + count)
    parts = [ref[cut, t * shard : (t + 1) * shard, :] for t in parts]
    parts = [part.reshape(count * shard, LANES) for part in parts]
    return jnp.concatenate(parts, axis=1)


def put_rows(ref, first, count, shard, rows):
    for t in range(rows.shape[1] // LANES):
        part = rows[:, t * LANES : (t + 1) * LANES].reshape(count, shard, LANES)
        ref[first : first + count, t * shard : (t + 1) * shard, :] = part


def row_places(phi_ref, first, shards, shard):
    out = []
    for k in range(shards):
        block = phi_ref[first + k]
        last = block.shape[0] - EXTRA
        code = to_rows(block[last : last + 1, :].astype(jnp.float32))
        out.append(code[:shard] * 256.0 + code[shard : 2 * shard])
    return jnp.concatenate(out, axis=0)


def hit_mask(places, base, ncol):
    rel = places - base
    lane = lax.broadcasted_iota(jnp.int32, rel.shape, 1).astype(jnp.float32)
    off = rel - lane
    return jnp.concatenate(
        [off == float(t * LANES) for t in range(ncol // LANES)], axis=1
    )


def pack_kernel(phi_in, pos_in, out_ref, block_ref, pos_ref, sems, sem):
    shard, width = phi_in.shape
    loads = [pltpu.make_async_copy(pos_in, pos_ref, sems.at[0])]
    for t in range(width // LANES):
        part = phi_in.at[:, t * LANES : (t + 1) * LANES]
        held = block_ref.at[t * shard : (t + 1) * shard]
        loads.append(pltpu.make_async_copy(part, held, sems.at[1 + t]))
    for load in loads:
        load.start()
    loads[0].wait()
    places = pos_ref[...]
    high = lax.shift_right_logical(places, 8)
    code = jnp.concatenate([high, places - high * 256], axis=1).astype(jnp.float32)
    last = block_ref.shape[0] - EXTRA
    block_ref[last:, :] = jnp.broadcast_to(code, (EXTRA, LANES)).astype(jnp.bfloat16)
    for load in loads[1:]:
        load.wait()
    copies = [
        pltpu.make_async_copy(block_ref, out_ref.at[k], sem.at[k])
        for k in range(out_ref.shape[0])
    ]
    for copy in copies:
        copy.start()
    for copy in copies:
        copy.wait()


def chunks_of(refs, shard):
    per = CHUNK // shard
    out = []
    for half, ref in enumerate(refs):
        for first in range(0, ref.shape[0], per):
            out.append((len(out), half, first, ref))
    return out


def line_of(place_ref, number, half, count):
    lines = CHUNK // LANES
    core = place_ref[2]
    whose = core if half == 0 else 1 - core
    return whose * (count // 2 * lines) + (number % (count // 2)) * lines


def row_lines(scale2, shard, phi_ref, psi):
    per = CHUNK // shard
    out = []
    for _, _, first, ref in chunks_of((phi_ref,), shard):
        rows = fold_rows(ref, first, per, shard)
        logits = nt(rows, psi) * scale2
        peak = jnp.max(logits, axis=1, keepdims=True)
        total = jnp.sum(jnp.exp2(logits - peak), axis=1, keepdims=True)
        lse = peak + jnp.log2(total)
        for t in range(CHUNK // LANES):
            out.append(to_lanes(lse[t * LANES : (t + 1) * LANES]))
    return jnp.concatenate(out, axis=0)


def own_rows_kernel(scale2, shard, place_ref, phi_ref, *refs):
    pieces = refs[:-4]
    line_ref, psi_out, psi_ref, sem = refs[-4:]
    place_shards(place_ref, pieces, psi_ref)
    copy = pltpu.make_async_copy(psi_ref, psi_out, sem)
    copy.start()
    line_ref[...] = row_lines(scale2, shard, phi_ref, psi_ref[...])
    copy.wait()


def all_rows_kernel(
    scale2, shard, place_ref, phi_ref, line_ref, psi_ref, row_ref
):
    count = line_ref.shape[0]
    npeer = row_ref.shape[0]
    core = place_ref[2]
    lines = row_lines(scale2, shard, phi_ref, psi_ref[...])
    for whose, part in ((core, line_ref[...]), (1 - core, lines)):
        at = pl.multiple_of(whose * count, count)
        row_ref[:, pl.ds(at, count), :] = jnp.broadcast_to(part[None], (npeer, count, LANES))


def cols_kernel(
    scale2, shard, place_ref, own_ref, other_ref, psi_in, col_ref, psi_ref, sem
):
    copy = pltpu.make_async_copy(psi_in, psi_ref, sem)
    copy.start()
    nz = col_ref.shape[0]
    ncol = psi_ref.shape[0]
    nline = ncol // LANES
    per = CHUNK // shard
    base = place_ref[1].astype(jnp.float32)
    lane = lax.broadcasted_iota(jnp.int32, (CHUNK, LANES), 1).astype(jnp.float32)
    copy.wait()
    psi = psi_ref[...]
    col_max = jnp.full((1, ncol), -1e30, jnp.float32)
    col_sum = jnp.zeros((1, ncol), jnp.float32)
    count = jnp.zeros((LANES, LANES), jnp.float32)
    hit_sum = jnp.zeros((1, ncol), jnp.float32)
    for _, _, first, phi_ref in chunks_of((own_ref, other_ref), shard):
        rows = fold_rows(phi_ref, first, per, shard)
        logits = nt(rows, psi) * scale2
        new_max = jnp.maximum(col_max, jnp.max(logits, axis=0, keepdims=True))
        part = jnp.sum(jnp.exp2(logits - new_max), axis=0, keepdims=True)
        col_sum = col_sum * jnp.exp2(col_max - new_max) + part
        col_max = new_max
        places = row_places(phi_ref, first, per, shard)
        hit = hit_mask(places, base, ncol)
        hit_sum = hit_sum + jnp.sum(jnp.where(hit, logits, 0.0), axis=0, keepdims=True)
        high = jnp.floor((places - base) * (1.0 / LANES))
        low = places - base - high * LANES
        high = jnp.where(high == lane, 1.0, 0.0).astype(jnp.bfloat16)
        low = jnp.where(low == lane, 1.0, 0.0).astype(jnp.bfloat16)
        count = count + tn(high, low)
    col_lse = col_max + jnp.log2(col_sum)
    for k, line in enumerate((col_lse, hit_sum)):
        for t in range(nline):
            cut = line[:, t * LANES : (t + 1) * LANES]
            at = 2 * k * nline + t
            col_ref[:, at : at + 1, :] = jnp.broadcast_to(cut[None], (nz, 1, LANES))
    col_ref[:, nline : 2 * nline, :] = jnp.broadcast_to(
        count[None, :nline, :], (nz, nline, LANES)
    )


def tail_rows(value, width):
    terms = jnp.broadcast_to(value, (1, width))
    first = terms.astype(jnp.bfloat16).astype(jnp.float32)
    second = (terms - first).astype(jnp.bfloat16).astype(jnp.float32)
    third = terms - first - second
    row = lax.broadcasted_iota(jnp.int32, (EXTRA, width), 0)
    full = jnp.where(
        row == 0, first, jnp.where(row == 1, second, jnp.where(row == 2, third, 0.0))
    )
    return full.astype(jnp.bfloat16)


def weights_kernel(
    scale, scale2, shard, place_ref, own_ref, other_ref, psi_in, rows_ref, others_ref, *refs
):
    cols_ref, gown_ref, gother_ref, w_ref, tail_ref, shift_ref, psi_ref, sem = refs
    copy = pltpu.make_async_copy(psi_in, psi_ref, sem)
    copy.start()
    ncol, width = psi_ref.shape
    plane = gown_ref.shape[0]
    per = CHUNK // shard
    nline = ncol // LANES
    base = place_ref[1].astype(jnp.float32)
    shift2 = math.log2(scale)

    row_parts = jnp.concatenate([rows_ref[...], others_ref[...]], axis=0)
    row_peak = jnp.max(row_parts, axis=0)
    row_lse = row_peak + jnp.log2(jnp.sum(jnp.exp2(row_parts - row_peak[None]), axis=0))
    tail_ref[...] = tail_rows(jnp.sum(row_lse, keepdims=True), LANES)
    shift_ref[...] = row_lse - shift2

    col_parts = cols_ref[:, :nline, :]
    col_peak = jnp.max(col_parts, axis=0)
    col_lse = col_peak + jnp.log2(jnp.sum(jnp.exp2(col_parts - col_peak[None]), axis=0))
    counts = jnp.sum(cols_ref[:, nline : 2 * nline, :], axis=0)
    hits = jnp.sum(cols_ref[:, 2 * nline :, :], axis=0)
    col_total = jnp.sum(counts * col_lse - 2.0 * hits, keepdims=True)
    last = gown_ref.shape[1] - EXTRA
    tail = jnp.broadcast_to(tail_rows(col_total, LANES)[None], (plane, EXTRA, LANES))
    line = col_lse - jnp.log2(counts) - shift2
    line = jnp.concatenate([line[t : t + 1] for t in range(nline)], axis=1)

    copy.wait()
    psi = psi_ref[...]
    chunks = chunks_of((own_ref, other_ref), shard)
    for number, half, first, phi_ref in chunks:
        rows = fold_rows(phi_ref, first, per, shard)
        logits = nt(rows, psi) * scale2
        at = line_of(place_ref, number, half, len(chunks))
        lse = jnp.concatenate(
            [to_rows(shift_ref[pl.ds(at + t, 1), :]) for t in range(CHUNK // LANES)],
            axis=0,
        )
        lse = jnp.concatenate([lse] * nline, axis=1)
        hit = hit_mask(row_places(phi_ref, first, per, shard), base, ncol)
        weights = jnp.exp2(logits - lse) + jnp.exp2(logits - line)
        weights = (weights - jnp.where(hit, 2.0 * scale, 0.0)).astype(jnp.bfloat16)
        w_ref[number * CHUNK : (number + 1) * CHUNK, :] = weights
        out_ref = gother_ref if half else gown_ref
        if (first + per) % GROUP == 0:
            end = (number + 1) * CHUNK
            part = nn(w_ref[end - GROUP * shard : end, :], psi).astype(jnp.bfloat16)
            put_rows(out_ref, first + per - GROUP, GROUP, shard, part)
    gown_ref[:, last:, :] = tail
    gother_ref[:, last:, :] = tail


def join_kernel(own_ref, other_ref, out, out_ref, sems):
    npeer = own_ref.shape[0]
    last = own_ref.shape[1] - EXTRA
    copies = []
    for k in range(npeer):
        total = own_ref[k].astype(jnp.float32) + other_ref[k].astype(jnp.float32)
        out_ref[k, :last, :] = total[:last].astype(jnp.bfloat16)
        if k == 0:
            loss = jnp.zeros((1, LANES), jnp.float32)
            for r in range(3):
                loss = loss + total[last + r : last + r + 1]
            tail = tail_rows(loss[:, :1], LANES)
        out_ref[k, last:, :] = tail
        if k % 4 == 3:
            cut = pl.ds(k - 3, 4)
            copies.append(
                pltpu.make_async_copy(out_ref.at[cut], out.at[cut], sems.at[k // 4])
            )
            copies[-1].start()
    for copy in copies:
        copy.wait()


def goals_kernel(shard, place_ref, w_ref, own_ref, other_ref, tail_ref, *refs):
    nz = 1 + len(SHIFTS)
    gpsi_refs = refs[:nz]
    (acc_ref,) = refs[nz:]
    nrow, ncol = w_ref.shape
    halves = [fold_rows(ref, 0, ref.shape[0], shard) for ref in (own_ref, other_ref)]
    rows = jnp.concatenate(halves, axis=0)
    for c in range(ncol // CHUNK):
        cut = slice(c * CHUNK, (c + 1) * CHUNK)
        acc_ref[cut, :] = tn(w_ref[:, cut], rows).astype(jnp.bfloat16)
    own = place_ref[0]
    piece = ncol // nz
    for out, shift in zip(gpsi_refs, (0,) + SHIFTS):
        slot = lax.rem(own + shift, nz)
        part = acc_ref[pl.ds(pl.multiple_of(slot * piece, piece), piece), :]
        for t in range(part.shape[1] // LANES):
            cut = slice(t * LANES, (t + 1) * LANES)
            out[t * piece : (t + 1) * piece, :] = part[:, cut]
        out[out.shape[0] - EXTRA :, :] = tail_ref[...]


def relay_kernel(parity, place_ref, *refs):
    out = refs[-1]
    piece = out.shape[0] - EXTRA
    width = out.shape[1]
    total = refs[0][...].astype(jnp.float32)
    for ref in refs[1:-2]:
        total = total + ref[...].astype(jnp.float32)
    counts = lax.rem(place_ref[0], 2) == parity
    total = total + jnp.where(counts, refs[-2][...].astype(jnp.float32), 0.0)
    out[:piece, :] = total[:piece].astype(jnp.bfloat16)
    loss = jnp.zeros((1, LANES), jnp.float32)
    for r in range(3):
        loss = loss + total[piece + r : piece + r + 1, :LANES]
    out[piece:, :] = tail_rows(loss[:, :1], width)


def total_kernel(nrow, phi_parts_ref, *refs):
    parts = refs[:-3]
    gphi_ref, gpsi_ref, loss_ref = refs[-3:]
    shard = gphi_ref.shape[0]
    piece = gpsi_ref.shape[0]
    total = phi_parts_ref[0].astype(jnp.float32)
    for k in range(1, phi_parts_ref.shape[0]):
        total = total + phi_parts_ref[k].astype(jnp.float32)
    for t in range(gphi_ref.shape[1] // LANES):
        gphi_ref[:, t * LANES : (t + 1) * LANES] = total[t * shard : (t + 1) * shard]
    last = total.shape[0] - EXTRA
    loss = total[last : last + 1]
    for r in range(1, 3):
        loss = loss + total[last + r : last + r + 1]
    total = parts[0][...].astype(jnp.float32)
    for part in parts[1:]:
        total = total + part[...].astype(jnp.float32)
    for t in range(gpsi_ref.shape[1] // LANES):
        gpsi_ref[:, t * LANES : (t + 1) * LANES] = total[t * piece : (t + 1) * piece]
    last = total.shape[0] - EXTRA
    for r in range(3):
        loss = loss + total[last + r : last + r + 1]
    loss_ref[...] = loss[:, :1] * (math.log(2.0) / nrow)


def shards(phi, psi, positives):
    shard, width = phi.shape
    piece = psi.shape[0]
    npeer = lax.axis_size(PEERS)
    nz = lax.axis_size("z")
    nrow = npeer * shard
    ncol = nz * piece
    scale = 1.0 / math.sqrt(width)
    scale2 = scale * LOG2E
    peer = lax.axis_index(PEERS)
    place = jnp.stack(
        [lax.axis_index("z"), peer * ncol, lax.axis_index("core")]
    ).astype(jnp.int32)

    def spread(array, axes):
        return lax.all_to_all(array, axes, 0, 0, tiled=True)

    def swap(array):
        return lax.ppermute(array, "core", [(0, 1), (1, 0)])

    def move(array, shift):
        return lax.ppermute(array, "z", [(i, (i + shift) % nz) for i in range(nz)])

    smem = pl.BlockSpec(memory_space=pltpu.SMEM)
    vmem = pl.BlockSpec(memory_space=pltpu.VMEM)
    hbm = pl.BlockSpec(memory_space=pltpu.HBM)
    params = pltpu.CompilerParams(vmem_limit_bytes=VMEM_LIMIT)

    nplane = npeer // 2
    fold = shard * width // LANES + EXTRA
    half = jax.ShapeDtypeStruct((nplane, fold, LANES), jnp.bfloat16)
    packed = pl.pallas_call(
        pack_kernel,
        out_shape=pltpu.HBM(half.shape, half.dtype),
        in_specs=[hbm] * 2,
        out_specs=hbm,
        scratch_shapes=[
            pltpu.VMEM(half.shape[1:], half.dtype),
            pltpu.VMEM((1, shard), jnp.int32),
            pltpu.SemaphoreType.DMA((1 + width // LANES,)),
            pltpu.SemaphoreType.DMA((nplane,)),
        ],
        compiler_params=params,
        name="pack",
    )(
        pltpu.with_memory_space_constraint(phi, pltpu.HBM),
        pltpu.with_memory_space_constraint(positives.reshape(1, shard), pltpu.HBM),
    )
    own = spread(packed, PLANE)
    near = {0: psi, 2: move(psi, 2), 6: move(psi, 6), 1: move(psi, 1), 7: move(psi, 7)}
    even = lax.rem(lax.axis_index("z"), 2) == 0
    across = [(i, (i + (2 if i % 2 == 0 else 6)) % nz) for i in range(nz)]
    near[4] = lax.ppermute(jnp.where(even, near[2], near[6]), "z", across)
    near[3] = move(near[2], 1)
    near[5] = move(near[6], 7)
    tied = lax.optimization_barrier((own, *[near[k] for k in range(nz)]))
    own = tied[0]
    near = dict(enumerate(tied[1:]))
    other = swap(own)
    goals = [near[k] for k in range(nz)]
    flops = 2 * nrow * ncol * width

    def cost(products):
        return pl.CostEstimate(
            flops=int(products * flops), bytes_accessed=4 << 20, transcendentals=int(products * nrow * ncol)
        )

    dma = pltpu.SemaphoreType.DMA
    psi_scratch = pltpu.VMEM((ncol, width), jnp.bfloat16)
    tile = jax.ShapeDtypeStruct((nrow, ncol), jnp.bfloat16)
    own_lines, psi_all, psi_near = pl.pallas_call(
        functools.partial(own_rows_kernel, scale2, shard),
        out_shape=(
            jax.ShapeDtypeStruct((nrow // LANES // 2, LANES), jnp.float32),
            pltpu.HBM((ncol, width), jnp.bfloat16),
            jax.ShapeDtypeStruct((ncol, width), jnp.bfloat16),
        ),
        in_specs=[smem] + [vmem] * (1 + nz),
        out_specs=(vmem, hbm, vmem),
        scratch_shapes=[dma],
        compiler_params=params,
        cost_estimate=cost(0.5),
        name="own_rows",
    )(place, own, *goals)
    psi_all = pltpu.with_memory_space_constraint(psi_all, pltpu.HBM)
    row_stats = pl.pallas_call(
        functools.partial(all_rows_kernel, scale2, shard),
        out_shape=jax.ShapeDtypeStruct((nplane, nrow // LANES, LANES), jnp.float32),
        in_specs=[smem] + [vmem] * 3,
        out_specs=vmem,
        compiler_params=params,
        cost_estimate=cost(0.5),
        name="all_rows",
    )(place, other, own_lines, psi_near)
    row_parts = spread(row_stats, PLANE)

    col_stats = pl.pallas_call(
        functools.partial(cols_kernel, scale2, shard),
        out_shape=jax.ShapeDtypeStruct((nz, 3 * ncol // LANES, LANES), jnp.float32),
        in_specs=[smem] + [vmem] * 2 + [hbm],
        out_specs=vmem,
        scratch_shapes=[psi_scratch, dma],
        compiler_params=params,
        cost_estimate=cost(1),
        name="cols",
    )(place, own, other, psi_all)
    row_parts, col_stats = lax.optimization_barrier((row_parts, col_stats))
    row_others = swap(row_parts)
    col_parts = spread(col_stats, "z")

    gown, gother, weights, tail = pl.pallas_call(
        functools.partial(weights_kernel, scale, scale2, shard),
        out_shape=(half, half, tile, jax.ShapeDtypeStruct((EXTRA, LANES), jnp.bfloat16)),
        in_specs=[smem] + [vmem] * 2 + [hbm] + [vmem] * 3,
        out_specs=(vmem,) * 4,
        scratch_shapes=[pltpu.VMEM((nrow // LANES, LANES), jnp.float32), psi_scratch, dma],
        compiler_params=params,
        cost_estimate=cost(2),
        name="weights",
    )(place, own, other, psi_all, row_parts, row_others, col_parts)
    part = jax.ShapeDtypeStruct((piece * width // LANES + EXTRA, LANES), jnp.bfloat16)
    gpsi = pl.pallas_call(
        functools.partial(goals_kernel, shard),
        out_shape=(part,) * nz,
        in_specs=[smem] + [vmem] * 4,
        out_specs=(vmem,) * nz,
        scratch_shapes=[pltpu.VMEM((ncol, width), jnp.bfloat16)],
        compiler_params=params,
        cost_estimate=cost(1),
        name="goals",
    )(place, weights, own, other, tail)

    other_part, *gpsi = lax.optimization_barrier((swap(gother), *gpsi))
    joined = pl.pallas_call(
        join_kernel,
        out_shape=pltpu.HBM(half.shape, half.dtype),
        in_specs=[vmem] * 2,
        out_specs=hbm,
        scratch_shapes=[pltpu.VMEM(half.shape, half.dtype), dma((nplane // 4,))],
        compiler_params=params,
        name="join",
    )(gown, other_part)
    phi_parts = spread(joined, PLANE)

    def relay(parity, *parts):
        return pl.pallas_call(
            functools.partial(relay_kernel, parity),
            out_shape=part,
            in_specs=[smem] + [vmem] * len(parts),
            out_specs=vmem,
            compiler_params=params,
            name="relay",
        )(place, *parts)

    over4 = lax.ppermute(gpsi[4], "z", across)
    over3, over5 = move(gpsi[3], 1), move(gpsi[5], 7)
    over3, over4, over5, up1, down1 = lax.optimization_barrier(
        (over3, over4, over5, gpsi[1], gpsi[7])
    )
    psi_parts = [gpsi[0], move(up1, 1), move(down1, 7)]
    psi_parts.append(move(relay(0, gpsi[2], over3, over4), 2))
    psi_parts.append(move(relay(1, gpsi[6], over5, over4), 6))

    grad_phi, grad_psi, loss = pl.pallas_call(
        functools.partial(total_kernel, nrow * nz),
        out_shape=(
            jax.ShapeDtypeStruct((shard, width), jnp.float32),
            jax.ShapeDtypeStruct((piece, width), jnp.float32),
            jax.ShapeDtypeStruct((1, 1), jnp.float32),
        ),
        in_specs=[vmem] * (1 + len(psi_parts)),
        out_specs=(vmem,) * 3,
        compiler_params=params,
        name="totals",
    )(phi_parts, *psi_parts)
    return (grad_phi, grad_psi, loss.reshape(()))


def solution(mesh):
    nrow, ngoal = mesh.shape["row"], mesh.shape["goal"]
    fine = Mesh(mesh.devices.reshape(nrow // 2, 2, ngoal // 8, 8), ALL)
    return jax.shard_map(
        shards,
        mesh=fine,
        in_specs=(P(ALL, None), P(ALL, None), P(ALL)),
        out_specs=(P(ALL, None), P(ALL, None), P()),
        check_vma=False,
    )
```
